128 devices in a mesh: prompt: 4 (over y_hi, core), resp: 32 (over x, z, y_lo).
Axes of the slice: x: 4, y: 4 (y_hi: 2, y_lo: 2; y = y_hi * 2 + y_lo), z: 4, core: 2. Of those that a mesh axis runs over, the one named last changes fastest.
Arguments:
- prompt_keys: bfloat16 [512, 1024], P(('prompt', 'resp')), may hold values from -6 to 6
- prompt_values: bfloat16 [512, 1024], P(('prompt', 'resp')), may hold values from -24 to 24
- resp_queries: bfloat16 [16384, 8192], P('resp', 'prompt'), may hold values from -6 to 6
- resp_keys: bfloat16 [16384, 1024], P('resp', 'prompt'), may hold values from -6 to 6
- resp_values: bfloat16 [16384, 1024], P('resp', 'prompt'), may hold values from -24 to 24
- grad_out: bfloat16 [16384, 8192], P('resp', 'prompt'), may hold values from -24 to 24
- lengths: int32 [32], replicated, may hold values from 128 to 512, as said below
Outputs:
- attended: bfloat16 [16384, 8192], P('resp', 'prompt')
- query_grads: bfloat16 [16384, 8192], P('resp', 'prompt')
- key_grads: bfloat16 [16384, 1024], P('resp', 'prompt')
- value_grads: bfloat16 [16384, 1024], P('resp', 'prompt')
- prompt_key_grads: bfloat16 [512, 1024], P(('prompt', 'resp'))
- prompt_value_grads: bfloat16 [512, 1024], P(('prompt', 'resp'))
The draws below stay inside these ranges and needn't reach their ends.
Inputs may be any that keep to these rules, and one draw needn't show every extreme that they name: `lengths`: each length is a multiple of 128, and some response has length 512 in every draw.
All inputs are finite; a program needn't handle non-finite values.
Results may differ from the reference program's by a relative error of at most 0.0092.
Values may be sent and summed in bfloat16 or wider, within the bound.
No kernel may reach another device: no remote copies, remote signals or barrier semaphores. Data moves between devices by JAX's collectives and lax.ppermute only.
A program may use at most 192 MiB of HBM per device.

```python
import math
import jax
import jax.numpy as jnp
from jax import lax

H = 64
KVH = 8
HD = 128
RLEN = 512
NRESP = 32
RTOT = 16384
PROMPT = 512


def draw_prompt_keys(key, part):
    key = jax.random.fold_in(key, 1)
    base = jnp.clip(jax.random.normal(key, (PROMPT, KVH * HD), jnp.float32), -6.0, 6.0)
    return base.astype(jnp.bfloat16)


def draw_resp_queries(key, part):
    key = jax.random.fold_in(key, 2)
    base = jnp.clip(1.5 * jax.random.normal(key, (RTOT, H * HD), jnp.float32), -6.0, 6.0)
    return base.astype(jnp.bfloat16)


def draw_lengths(key, part):
    key = jax.random.fold_in(key, 3)
    first, second = jax.random.split(key)
    quarters = jax.random.randint(first, (NRESP,), 1, 5)
    chosen = jax.random.randint(second, (), 0, NRESP)
    quarters = jnp.where(jnp.arange(NRESP) == chosen, 4, quarters)
    return (quarters * (RLEN // 4)).astype(jnp.int32)


def block_scale(own_key, extent, pieces, least, largest):
    def one(dim, blocks):
        steps = jax.random.uniform(jax.random.fold_in(jax.random.fold_in(own_key, 6), dim), (blocks,), jnp.float32, least / len(pieces), largest / len(pieces))
        return jnp.repeat(jnp.exp(steps), extent[dim] // blocks).reshape((-1,) + (1,) * (len(extent) - dim - 1))

    gain = one(*pieces[0])
    for cut in pieces[1:]:
        gain = gain * one(*cut)
    return gain


def centred(rng, dims, spread, most, shards=(), dtype=jnp.bfloat16):
    gain = block_scale(rng, dims, shards, -0.22, 0.18) if shards else 1.0
    entries = jax.random.normal(rng, dims, jnp.float32) * spread * gain
    return jnp.minimum(jnp.maximum(entries, -most), most).astype(dtype)


def setup_inputs(seed: int = 0) -> dict:
    key_of = jax.random.split(jax.random.key(seed), 8)
    prompt_keys = draw_prompt_keys(jax.random.fold_in(key_of[7], 71), 0)
    prompt_values = centred(key_of[1], (PROMPT, KVH * HD), 4.0, 24.0, ((0, 128),))
    resp_queries = draw_resp_queries(jax.random.fold_in(key_of[7], 71), 0)
    resp_keys = centred(key_of[3], (RTOT, KVH * HD), 1.0, 6.0, ((0, 32), (1, 4)))
    resp_values = centred(key_of[4], (RTOT, KVH * HD), 4.0, 24.0, ((0, 32), (1, 4)))
    grad_out = centred(key_of[5], (RTOT, H * HD), 4.0, 24.0, ((0, 32), (1, 4)))
    lengths = draw_lengths(jax.random.fold_in(key_of[7], 71), 0)
    return {"prompt_keys": prompt_keys, "prompt_values": prompt_values, "resp_queries": resp_queries, "resp_keys": resp_keys, "resp_values": resp_values, "grad_out": grad_out, "lengths": lengths}


def group_pass(queries, keys, values, grads, allowed, live, scale):
    query_wide = queries.astype(jnp.float32)
    key_wide = keys.astype(jnp.float32)
    value_wide = values.astype(jnp.float32)
    grad_wide = grads.astype(jnp.float32)
    scores = jnp.einsum('thd,kd->thk', query_wide, key_wide) * scale
    scores = jnp.where(allowed[:, None, :], scores, -1e+30)
    peak = lax.optimization_barrier(jnp.max(scores, axis=2, keepdims=True))
    exponent = jnp.exp(scores - peak)
    probs = exponent / lax.optimization_barrier(jnp.sum(exponent, axis=2, keepdims=True))
    weights = probs.astype(jnp.bfloat16)
    mixed = jnp.einsum('thk,kd->thd', weights.astype(jnp.float32), value_wide)
    attended = jnp.where(live[:, None, None], mixed, 0.0).astype(jnp.bfloat16)
    drift = lax.optimization_barrier(jnp.sum(grad_wide * mixed, axis=2, keepdims=True))
    prob_grads = jnp.einsum('thd,kd->thk', grad_wide, value_wide)
    score_grads = (probs * (prob_grads - drift) * scale).astype(jnp.bfloat16)
    score_wide = score_grads.astype(jnp.float32)
    query_grads = jnp.einsum('thk,kd->thd', score_wide, key_wide).astype(jnp.bfloat16)
    key_grads = jnp.einsum('thk,thd->kd', score_wide, query_wide)
    value_grads = jnp.einsum('thk,thd->kd', weights.astype(jnp.float32), grad_wide)
    return (attended, query_grads, key_grads, value_grads)

def reference(prompt_keys, prompt_values, resp_queries, resp_keys, resp_values, grad_out, lengths):
    scale = 1.0 / math.sqrt(HD)
    per_group = H // KVH
    offsets = jnp.arange(RLEN)
    allowed = jnp.concatenate([jnp.ones((RLEN, PROMPT), bool), offsets[None, :] <= offsets[:, None]], axis=1)

    def one_response(carry, inputs):
        queries_all, keys_all, values_all, grads_all, length = inputs
        live = offsets < length
        masked = jnp.where(live[:, None], grads_all, jnp.zeros_like(grads_all))
        attended_parts, query_parts = ([], [])
        prompt_kg, prompt_vg, own_kg, own_vg = ([], [], [], [])
        for group in range(KVH):
            query_cols = slice(group * per_group * HD, (group + 1) * per_group * HD)
            key_cols = slice(group * HD, (group + 1) * HD)
            queries = queries_all[:, query_cols].reshape(RLEN, per_group, HD)
            grads = masked[:, query_cols].reshape(RLEN, per_group, HD)
            keys = jnp.concatenate([prompt_keys[:, key_cols], keys_all[:, key_cols]], axis=0)
            values = jnp.concatenate([prompt_values[:, key_cols], values_all[:, key_cols]], axis=0)
            attended, query_grads, key_grads, value_grads = group_pass(queries, keys, values, grads, allowed, live, scale)
            attended_parts.append(attended.reshape(RLEN, per_group * HD))
            query_parts.append(query_grads.reshape(RLEN, per_group * HD))
            prompt_kg.append(key_grads[:PROMPT])
            prompt_vg.append(value_grads[:PROMPT])
            own_kg.append(key_grads[PROMPT:])
            own_vg.append(value_grads[PROMPT:])
        new_carry = (carry[0] + jnp.concatenate(prompt_kg, axis=1), carry[1] + jnp.concatenate(prompt_vg, axis=1))
        results = (jnp.concatenate(attended_parts, axis=1), jnp.concatenate(query_parts, axis=1), jnp.concatenate(own_kg, axis=1).astype(jnp.bfloat16), jnp.concatenate(own_vg, axis=1).astype(jnp.bfloat16))
        return (new_carry, results)
    inputs = (resp_queries.reshape(NRESP, RLEN, H * HD), resp_keys.reshape(NRESP, RLEN, KVH * HD), resp_values.reshape(NRESP, RLEN, KVH * HD), grad_out.reshape(NRESP, RLEN, H * HD), lengths)
    start = jnp.zeros((PROMPT, KVH * HD), jnp.float32)
    sums, results = lax.scan(one_response, (start, start), inputs)
    attended, query_grads, key_grads, value_grads = results
    return (attended.reshape(RTOT, H * HD), query_grads.reshape(RTOT, H * HD), key_grads.reshape(RTOT, KVH * HD), value_grads.reshape(RTOT, KVH * HD), sums[0].astype(jnp.bfloat16), sums[1].astype(jnp.bfloat16))
```

```python
import functools
import math

import jax
import jax.numpy as jnp
from jax import lax
from jax.experimental import pallas as pl
from jax.experimental.pallas import tpu as pltpu
from jax.sharding import PartitionSpec as P

HD = 128
BLK = 256
SCALE = 1.0 / math.sqrt(HD)
EXP_SCALE = SCALE * math.log2(math.e)
NEG = -1e30
F32 = jnp.float32
BF16 = jnp.bfloat16


def dot_nt(a, b):
    return lax.dot_general(a, b, (((1,), (1,)), ((), ())), preferred_element_type=F32)


def dot_nn(a, b):
    return lax.dot_general(a, b, (((1,), (0,)), ((), ())), preferred_element_type=F32)


def live_rows(block, start, length):
    parts = []
    for at in range(0, block.shape[0], HD):
        factor = (start + at < length).astype(F32).astype(BF16)
        parts.append(block[at : at + HD] * factor)
    return jnp.concatenate(parts, axis=0)


def causal(s):
    key = lax.broadcasted_iota(jnp.int32, s.shape, 0)
    query = lax.broadcasted_iota(jnp.int32, s.shape, 1)
    return jnp.where(key <= query, s, NEG)


def own_scores(k, q, at):
    s = dot_nt(k[: at + BLK], q)
    tail = causal(s[at:])
    return tail if at == 0 else jnp.concatenate([s[:at], tail], axis=0)


def own_forward(q_ref, k_ref, v_ref, mixed_ref, stats_ref, vt_ref, *, per_group):
    @pl.when(pl.program_id(0) % per_group == 0)
    def _():
        vt_ref[...] = v_ref[...].T

    rows = q_ref.shape[0]
    for at in range(0, rows, BLK):
        s = own_scores(k_ref[...], q_ref[at : at + BLK, :], at)
        peak = jnp.max(s, axis=0, keepdims=True)
        e = jnp.exp2((s - peak) * EXP_SCALE)
        total = jnp.sum(e, axis=0, keepdims=True)
        mixed_ref[0, :, at : at + BLK] = dot_nn(vt_ref[:, : at + BLK], e.astype(BF16))
        stats_ref[0, 0:1, at : at + BLK] = peak
        stats_ref[0, 1:2, at : at + BLK] = total


def shared_pass(
    length_ref, q_ref, g_ref, k_ref, v_ref, mixed_ref, stats_ref,
    att_ref, qg_ref, back_ref, kg_ref, vg_ref, kt_ref, vt_ref, *, per_group
):
    length = length_ref[0]
    rows = q_ref.shape[0]

    @pl.when(pl.program_id(0) % per_group == 0)
    def _():
        kt_ref[...] = k_ref[0].T
        vt_ref[...] = v_ref[0].T
        kg_ref[...] = jnp.zeros_like(kg_ref)
        vg_ref[...] = jnp.zeros_like(vg_ref)

    keys, values = k_ref[0], v_ref[0]
    for at in range(0, rows, BLK):
        cols = slice(at, at + BLK)
        q = q_ref[cols, :]
        g = live_rows(g_ref[cols, :], at, length)
        s = dot_nt(keys, q)
        own_peak = stats_ref[0, 0:1, cols]
        peak = jnp.maximum(jnp.max(s, axis=0, keepdims=True), own_peak)
        e = jnp.exp2((s - peak) * EXP_SCALE)
        decay = jnp.exp2((own_peak - peak) * EXP_SCALE)
        total = jnp.sum(e, axis=0, keepdims=True) + stats_ref[0, 1:2, cols] * decay
        inverse = 1.0 / total
        p = e * inverse
        w = p.astype(BF16)
        mixed = dot_nn(vt_ref[...], w) + mixed_ref[0, :, cols] * (decay * inverse)
        live = lax.broadcasted_iota(jnp.int32, (1, BLK), 1) + at < length
        att_ref[cols, :] = jnp.where(live, mixed, 0.0).T.astype(BF16)
        drift = jnp.sum(g.T.astype(F32) * mixed, axis=0, keepdims=True)
        dp = dot_nt(values, g)
        ds = (p * (dp - drift) * SCALE).astype(BF16)
        qg_ref[0, :, cols] = dot_nn(kt_ref[...], ds)
        kg_ref[0] += dot_nn(ds, q)
        vg_ref[0] += dot_nn(w, g)
        back_ref[0, 0:1, cols] = peak
        back_ref[0, 1:2, cols] = inverse
        back_ref[0, 2:3, cols] = drift


def own_backward(
    length_ref, q_ref, g_ref, k_ref, v_ref, part_ref, back_ref,
    qg_ref, kg_ref, vg_ref, kt_ref, kacc_ref, vacc_ref, *, per_group
):
    length = length_ref[0]
    rows = q_ref.shape[0]
    head = pl.program_id(0) % per_group

    @pl.when(head == 0)
    def _():
        kt_ref[...] = k_ref[...].T
        kacc_ref[...] = jnp.zeros_like(kacc_ref)
        vacc_ref[...] = jnp.zeros_like(vacc_ref)

    for at in range(0, rows, BLK):
        cols = slice(at, at + BLK)
        upto = slice(0, at + BLK)
        q = q_ref[cols, :]
        g = live_rows(g_ref[cols, :], at, length)
        s = own_scores(k_ref[...], q, at)
        p = jnp.exp2((s - back_ref[0, 0:1, cols]) * EXP_SCALE) * back_ref[0, 1:2, cols]
        w = p.astype(BF16)
        dp = dot_nt(v_ref[upto, :], g)
        ds = (p * (dp - back_ref[0, 2:3, cols]) * SCALE).astype(BF16)
        qg = dot_nn(kt_ref[:, upto], ds) + part_ref[0, :, cols]
        qg_ref[cols, :] = qg.T.astype(BF16)
        kacc_ref[upto, :] += dot_nn(ds, q)
        vacc_ref[upto, :] += dot_nn(w, g)

    @pl.when(head == per_group - 1)
    def _():
        kg_ref[...] = kacc_ref[...].astype(BF16)
        vg_ref[...] = vacc_ref[...].astype(BF16)


VMEM_LIMIT = 48 * 2**20


def params():
    return pltpu.CompilerParams(
        dimension_semantics=("arbitrary",), vmem_limit_bytes=VMEM_LIMIT
    )


def shape(dims, dtype=F32):
    return jax.ShapeDtypeStruct(dims, dtype)


def run_own_forward(q, k, v):
    rows, width = q.shape
    heads, groups = width // HD, k.shape[1] // HD
    per_group = heads // groups
    return pl.pallas_call(
        functools.partial(own_forward, per_group=per_group),
        grid=(heads,),
        in_specs=[
            pl.BlockSpec((rows, HD), lambda h: (0, h)),
            pl.BlockSpec((rows, HD), lambda h: (0, h // per_group)),
            pl.BlockSpec((rows, HD), lambda h: (0, h // per_group)),
        ],
        out_specs=[
            pl.BlockSpec((1, HD, rows), lambda h: (h, 0, 0)),
            pl.BlockSpec((1, 8, rows), lambda h: (h, 0, 0)),
        ],
        out_shape=[shape((heads, HD, rows)), shape((heads, 8, rows))],
        scratch_shapes=[pltpu.VMEM((HD, rows), BF16)],
        compiler_params=params(),
        cost_estimate=pl.CostEstimate(
            flops=3 * heads * rows * rows * HD, bytes_accessed=8 * 2**20, transcendentals=0
        ),
        name="own_forward",
    )(q, k, v)


def run_shared(length, q, g, k, v, mixed, stats):
    rows, width = q.shape
    heads, groups = width // HD, k.shape[0]
    near = k.shape[1]
    per_group = heads // groups
    head_block = pl.BlockSpec((rows, HD), lambda h: (0, h))
    group_block = pl.BlockSpec((1, near, HD), lambda h: (h // per_group, 0, 0))
    wide_block = pl.BlockSpec((1, HD, rows), lambda h: (h, 0, 0))
    stat_block = pl.BlockSpec((1, 8, rows), lambda h: (h, 0, 0))
    return pl.pallas_call(
        functools.partial(shared_pass, per_group=per_group),
        grid=(heads,),
        in_specs=[
            pl.BlockSpec(memory_space=pltpu.SMEM),
            head_block, head_block, group_block, group_block, wide_block, stat_block,
        ],
        out_specs=[head_block, wide_block, stat_block, group_block, group_block],
        out_shape=[
            shape((rows, width), BF16), shape((heads, HD, rows)), shape((heads, 8, rows)),
            shape((groups, near, HD)), shape((groups, near, HD)),
        ],
        scratch_shapes=[pltpu.VMEM((HD, near), BF16)] * 2,
        compiler_params=params(),
        cost_estimate=pl.CostEstimate(
            flops=12 * heads * rows * near * HD, bytes_accessed=16 * 2**20, transcendentals=0
        ),
        name="shared_pass",
    )(length, q, g, k, v, mixed, stats)


def run_own_backward(length, q, g, k, v, part, back):
    rows, width = q.shape
    heads, groups = width // HD, k.shape[1] // HD
    per_group = heads // groups
    head_block = pl.BlockSpec((rows, HD), lambda h: (0, h))
    group_block = pl.BlockSpec((rows, HD), lambda h: (0, h // per_group))
    return pl.pallas_call(
        functools.partial(own_backward, per_group=per_group),
        grid=(heads,),
        in_specs=[
            pl.BlockSpec(memory_space=pltpu.SMEM),
            head_block, head_block, group_block, group_block,
            pl.BlockSpec((1, HD, rows), lambda h: (h, 0, 0)),
            pl.BlockSpec((1, 8, rows), lambda h: (h, 0, 0)),
        ],
        out_specs=[head_block, group_block, group_block],
        out_shape=[shape((rows, width), BF16), shape(k.shape, BF16), shape(v.shape, BF16)],
        scratch_shapes=[
            pltpu.VMEM((HD, rows), BF16), pltpu.VMEM((rows, HD), F32), pltpu.VMEM((rows, HD), F32)
        ],
        compiler_params=params(),
        cost_estimate=pl.CostEstimate(
            flops=8 * heads * rows * rows * HD, bytes_accessed=12 * 2**20, transcendentals=0
        ),
        name="own_backward",
    )(length, q, g, k, v, part, back)


def on_device(prompt_keys, prompt_values, q, resp_k, resp_v, grad_out, lengths):
    axes = ("prompt", "resp")
    shares = lax.axis_size("prompt")
    copies = lax.axis_size("resp")
    tokens = prompt_keys.shape[0]
    groups = resp_k.shape[1] // HD
    near = tokens * shares * copies
    length = lax.dynamic_slice(lengths, (lax.axis_index("resp"),), (1,))

    pieces = jnp.stack([prompt_keys, prompt_values], axis=1)
    pieces = pieces.reshape(tokens, 2, shares, groups, HD).transpose(2, 0, 1, 3, 4)
    pieces = jnp.broadcast_to(pieces[:, None], (shares, copies) + pieces.shape[1:])
    pieces = pieces.reshape(shares * copies, tokens * 2 * groups, HD)
    arrived = lax.all_to_all(pieces, axes, split_axis=0, concat_axis=0, tiled=True)
    arrived = arrived.reshape(near, 2, groups, HD).transpose(1, 2, 0, 3)

    mixed, stats = run_own_forward(q, resp_k, resp_v)
    attended, part, back, kg, vg = run_shared(
        length, q, grad_out, arrived[0], arrived[1], mixed, stats
    )
    terms = jnp.stack([kg, vg]).transpose(2, 0, 1, 3).astype(BF16)
    terms = terms.reshape(shares * copies, tokens * 2 * groups, HD)
    terms = lax.all_to_all(terms, axes, split_axis=0, concat_axis=0, tiled=True)
    query_grads, key_grads, value_grads = run_own_backward(
        length, q, grad_out, resp_k, resp_v, part, back
    )
    terms = terms.reshape(shares, copies, tokens, 2, groups, HD).astype(F32)
    sums = jnp.sum(terms, axis=1).transpose(2, 1, 0, 3, 4)
    sums = sums.reshape(2, tokens, shares * groups * HD).astype(BF16)
    return attended, query_grads, key_grads, value_grads, sums[0], sums[1]


def solution(mesh):
    return jax.shard_map(
        on_device,
        mesh=mesh,
        in_specs=(
            P(("prompt", "resp"), None),
            P(("prompt", "resp"), None),
            P("resp", "prompt"),
            P("resp", "prompt"),
            P("resp", "prompt"),
            P("resp", "prompt"),
            P(),
        ),
        out_specs=(
            P("resp", "prompt"),
            P("resp", "prompt"),
            P("resp", "prompt"),
            P("resp", "prompt"),
            P(("prompt", "resp"), None),
            P(("prompt", "resp"), None),
        ),
        check_vma=False,
    )
```

```python
import functools
import math

import jax
import jax.numpy as jnp
from jax import lax
from jax.experimental import pallas as pl
from jax.experimental.pallas import tpu as pltpu
from jax.sharding import PartitionSpec as P

HD = 128
BLK = 256
SCALE = 1.0 / math.sqrt(HD)
EXP_SCALE = SCALE * math.log2(math.e)
NEG = -1e30
F32 = jnp.float32
BF16 = jnp.bfloat16


def dot_nt(a, b):
    return lax.dot_general(a, b, (((1,), (1,)), ((), ())), preferred_element_type=F32)


def dot_nn(a, b):
    return lax.dot_general(a, b, (((1,), (0,)), ((), ())), preferred_element_type=F32)


def live_rows(block, start, length):
    parts = []
    for at in range(0, block.shape[0], HD):
        factor = (start + at < length).astype(F32).astype(BF16)
        parts.append(block[at : at + HD] * factor)
    return jnp.concatenate(parts, axis=0)


def causal(s):
    key = lax.broadcasted_iota(jnp.int32, s.shape, 0)
    query = lax.broadcasted_iota(jnp.int32, s.shape, 1)
    return jnp.where(key <= query, s, NEG)


def stacked(ref, head):
    return ref[:, head * HD : (head + 1) * HD]


def own_forward(q_ref, k_ref, v_ref, mixed_ref, stats_ref, vt_ref, s_refs, w_refs, *, per_group):
    heads = mixed_ref.shape[0]
    rows = q_ref.shape[0]

    @pl.when(pl.program_id(0) % (per_group // heads) == 0)
    def _():
        vt_ref[...] = v_ref[...].T

    def scores(u):
        q = stacked(q_ref, u)
        for at in range(0, rows, BLK):
            end = at + BLK
            s_refs[u % 2][:end, at:end] = dot_nt(k_ref[:end, :], q[at:end])

    def mix(u):
        s_ref, w_ref = s_refs[u % 2], w_refs[u % 2]
        for at in range(0, rows, BLK):
            end = at + BLK
            tail = causal(s_ref[at:end, at:end])
            peak = jnp.max(tail, axis=0, keepdims=True)
            if at:
                peak = jnp.maximum(peak, jnp.max(s_ref[:at, at:end], axis=0, keepdims=True))
            e = jnp.exp2((tail - peak) * EXP_SCALE)
            total = jnp.sum(e, axis=0, keepdims=True)
            w_ref[at:end, at:end] = e.astype(BF16)
            if at:
                e = jnp.exp2((s_ref[:at, at:end] - peak) * EXP_SCALE)
                total += jnp.sum(e, axis=0, keepdims=True)
                w_ref[:at, at:end] = e.astype(BF16)
            mixed_ref[u, :, at:end] = dot_nn(vt_ref[:, :end], w_ref[:end, at:end])
            stats_ref[u, 0:1, at:end] = peak
            stats_ref[u, 1:2, at:end] = total

    for step in range(heads + 1):
        if step < heads:
            scores(step)
        if step:
            mix(step - 1)


def shared_pass(
    lengths_ref, q_ref, g_ref, near_ref, mixed_ref, stats_ref,
    att_ref, qg_ref, back_ref, terms_ref,
    near_wide, k_ref, v_ref, kt_ref, vt_ref, kg_ref, vg_ref, s_refs, dp_refs, w_refs, ds_refs,
    *, per_group
):
    length = lengths_ref[lax.axis_index("resp")]
    heads = mixed_ref.shape[0]
    rows = q_ref.shape[0]
    groups, near = k_ref.shape[:2]
    senders, chunk = near_ref.shape[:2]
    tokens = near // senders
    steps = per_group // heads
    step_id = pl.program_id(0)
    group = step_id // steps

    @pl.when(step_id == 0)
    def _():
        near_wide[...] = near_ref[...].astype(F32).reshape(senders * chunk, HD)
        for which, (ref, t_ref) in enumerate(((k_ref, kt_ref), (v_ref, vt_ref))):
            for one in range(groups):
                for token in range(tokens):
                    row = (which * groups + one) * tokens + token
                    piece = near_wide[pl.ds(row, senders, stride=chunk), :].astype(BF16)
                    ref[one, token * senders : (token + 1) * senders, :] = piece
                t_ref[one] = ref[one].T

    @pl.when(step_id % steps == 0)
    def _():
        kg_ref[...] = jnp.zeros_like(kg_ref)
        vg_ref[...] = jnp.zeros_like(vg_ref)

    peaks, inverses, drifts, scaled = {}, {}, {}, {}

    def grads(u):
        return live_rows(stacked(g_ref, u), 0, length)

    def scores(u):
        s = dot_nt(k_ref[group], stacked(q_ref, u))
        s_refs[u % 3][...] = s
        peaks[u] = jnp.maximum(jnp.max(s, axis=0, keepdims=True), stats_ref[u, 0:1, :])
        dp_refs[u % 3][...] = dot_nt(v_ref[group], grads(u))

    def mix(u):
        s_ref, w_ref = s_refs[u % 3], w_refs[u % 3]
        e = jnp.exp2((s_ref[...] - peaks[u]) * EXP_SCALE)
        s_ref[...] = e
        decay = jnp.exp2((stats_ref[u, 0:1, :] - peaks[u]) * EXP_SCALE)
        total = jnp.sum(e, axis=0, keepdims=True) + stats_ref[u, 1:2, :] * decay
        inverses[u] = 1.0 / total
        w_ref[...] = (s_ref[...] * inverses[u]).astype(BF16)
        mixed = dot_nn(vt_ref[group], w_ref[...]) + mixed_ref[u] * (decay * inverses[u])
        live = lax.broadcasted_iota(jnp.int32, (1, rows), 1) < length
        att_ref[:, u * HD : (u + 1) * HD] = jnp.where(live, mixed, 0.0).T.astype(BF16)
        drifts[u] = jnp.sum(grads(u).T.astype(F32) * mixed, axis=0, keepdims=True)
        back_ref[u, 0:1, :] = peaks[u]
        back_ref[u, 1:2, :] = inverses[u]
        back_ref[u, 2:3, :] = drifts[u]

    def spread(u):
        s_ref, dp_ref, w_ref, ds_ref = s_refs[u % 3], dp_refs[u % 3], w_refs[u % 3], ds_refs[u % 2]
        ds = s_ref[...] * (dp_ref[...] - drifts[u]) * (inverses[u] * SCALE)
        ds_ref[...] = ds.astype(BF16)
        qg_ref[u] = dot_nn(kt_ref[group], ds_ref[...])
        kg_ref[...] += dot_nn(ds_ref[...], stacked(q_ref, u))
        vg_ref[...] += dot_nn(w_ref[...], grads(u))

    for step in range(heads + 2):
        if step < heads:
            scores(step)
        if 0 <= step - 1 < heads:
            mix(step - 1)
        if step >= 2:
            spread(step - 2)

    for one in range(groups):
        @pl.when(step_id == (one + 1) * steps - 1)
        def _():
            for which, ref in enumerate((kg_ref, vg_ref)):
                for token in range(tokens):
                    row = (which * groups + one) * tokens + token
                    near_wide[pl.ds(row, senders, stride=chunk), :] = ref[
                        token * senders : (token + 1) * senders, :
                    ]

    @pl.when(step_id == groups * steps - 1)
    def _():
        terms_ref[...] = near_wide[...].reshape(senders, chunk, HD).astype(BF16)


def own_backward(
    lengths_ref, q_ref, g_ref, k_ref, v_ref, part_ref, back_ref,
    qg_ref, kg_ref, vg_ref, kt_ref, kacc_ref, vacc_ref, s_refs, dp_refs, w_refs, ds_refs,
    *, per_group
):
    length = lengths_ref[lax.axis_index("resp")]
    heads = part_ref.shape[0]
    rows = q_ref.shape[0]
    steps = per_group // heads
    turn = pl.program_id(0) % steps

    @pl.when(turn == 0)
    def _():
        kt_ref[...] = k_ref[...].T
        kacc_ref[...] = jnp.zeros_like(kacc_ref)
        vacc_ref[...] = jnp.zeros_like(vacc_ref)

    def scores(u):
        q = stacked(q_ref, u)
        g = live_rows(stacked(g_ref, u), 0, length)
        for at in range(0, rows, BLK):
            end = at + BLK
            s_refs[u % 2][:end, at:end] = dot_nt(k_ref[:end, :], q[at:end])
            dp_refs[u % 2][:end, at:end] = dot_nt(v_ref[:end, :], g[at:end])

    def spread(u):
        s_ref, dp_ref, w_ref, ds_ref = (refs[u % 2] for refs in (s_refs, dp_refs, w_refs, ds_refs))
        q = stacked(q_ref, u)
        g = live_rows(stacked(g_ref, u), 0, length)
        for at in range(0, rows, BLK):
            end = at + BLK
            peak = back_ref[u, 0:1, at:end]
            inverse = back_ref[u, 1:2, at:end]
            drift = back_ref[u, 2:3, at:end]
            for low in range(0, end, BLK):
                keys = slice(low, low + BLK)
                s = s_ref[keys, at:end]
                if low == at:
                    s = causal(s)
                p = jnp.exp2((s - peak) * EXP_SCALE) * inverse
                w_ref[keys, at:end] = p.astype(BF16)
                ds_ref[keys, at:end] = (p * (dp_ref[keys, at:end] - drift) * SCALE).astype(BF16)
            qg = dot_nn(kt_ref[:, :end], ds_ref[:end, at:end]) + part_ref[u, :, at:end]
            qg_ref[at:end, u * HD : (u + 1) * HD] = qg.T.astype(BF16)
        for low in range(0, rows, BLK):
            keys = slice(low, low + BLK)
            kacc_ref[keys, :] += dot_nn(ds_ref[keys, low:], q[low:])
            vacc_ref[keys, :] += dot_nn(w_ref[keys, low:], g[low:])

    for step in range(heads + 1):
        if step < heads:
            scores(step)
        if step:
            spread(step - 1)

    @pl.when(turn == steps - 1)
    def _():
        kg_ref[...] = kacc_ref[...].astype(BF16)
        vg_ref[...] = vacc_ref[...].astype(BF16)


def copy_pieces(k_ref, v_ref, out_ref):
    tokens, width = k_ref.shape
    shares, copies = out_ref.shape[:2]
    groups = width // shares // HD
    for share in range(shares):
        parts = []
        for ref in (k_ref, v_ref):
            for one in range(groups):
                at = (share * groups + one) * HD
                parts.append(ref[:, at : at + HD].astype(F32))
        piece = jnp.concatenate(parts, axis=0).astype(BF16)
        out_ref[share] = jnp.broadcast_to(piece[None], (copies,) + piece.shape)


def add_terms(terms_ref, k_ref, v_ref):
    tokens, width = k_ref.shape
    shares = terms_ref.shape[0]
    groups = width // shares // HD
    for share in range(shares):
        total = jnp.sum(terms_ref[share].astype(F32), axis=0)
        for which, ref in enumerate((k_ref, v_ref)):
            for one in range(groups):
                row = (which * groups + one) * tokens
                at = (share * groups + one) * HD
                ref[:, at : at + HD] = total[row : row + tokens].astype(BF16)


VMEM_LIMIT = 60 * 2**20
TURN = 4


def params():
    return pltpu.CompilerParams(
        dimension_semantics=("arbitrary",), vmem_limit_bytes=VMEM_LIMIT
    )


def shape(dims, dtype=F32):
    return jax.ShapeDtypeStruct(dims, dtype)


def specs(rows, per_group):
    steps = per_group // TURN
    return (
        pl.BlockSpec((rows, TURN * HD), lambda h: (0, h)),
        pl.BlockSpec((rows, HD), lambda h: (0, h // steps)),
        pl.BlockSpec((TURN, HD, rows), lambda h: (h, 0, 0)),
        pl.BlockSpec((TURN, 8, rows), lambda h: (h, 0, 0)),
    )


def cost(heads, rows, keys, matmuls, mib):
    return pl.CostEstimate(
        flops=2 * matmuls * heads * rows * keys * HD,
        bytes_accessed=mib * 2**20,
        transcendentals=heads * rows * keys,
    )


def run_own_forward(q, k, v):
    rows, width = q.shape
    heads, groups = width // HD, k.shape[1] // HD
    head, group, wide, stat = specs(rows, heads // groups)
    return pl.pallas_call(
        functools.partial(own_forward, per_group=heads // groups),
        grid=(heads // TURN,),
        in_specs=[head, group, group],
        out_specs=[wide, stat],
        out_shape=[shape((heads, HD, rows)), shape((heads, 8, rows))],
        scratch_shapes=[
            pltpu.VMEM((HD, rows), BF16),
            [pltpu.VMEM((rows, rows), F32)] * 2,
            [pltpu.VMEM((rows, rows), BF16)] * 2,
        ],
        compiler_params=params(),
        cost_estimate=cost(heads, rows, rows, 2, 8),
        name="own_forward",
    )(q, k, v)


def run_shared(lengths, q, g, arrived, mixed, stats):
    rows, width = q.shape
    heads = width // HD
    senders, chunk = arrived.shape[:2]
    groups = 2
    near = senders * chunk // (2 * groups)
    head, _, wide, stat = specs(rows, heads // groups)
    whole = pl.BlockSpec(arrived.shape, lambda h: (0, 0, 0))
    return pl.pallas_call(
        functools.partial(shared_pass, per_group=heads // groups),
        grid=(heads // TURN,),
        in_specs=[pl.BlockSpec(memory_space=pltpu.SMEM), head, head, whole, wide, stat],
        out_specs=[head, wide, stat, whole],
        out_shape=[
            shape((rows, width), BF16), shape((heads, HD, rows)), shape((heads, 8, rows)),
            shape(arrived.shape, BF16),
        ],
        scratch_shapes=[
            pltpu.VMEM((senders * chunk, HD), F32),
            pltpu.VMEM((groups, near, HD), BF16),
            pltpu.VMEM((groups, near, HD), BF16),
            pltpu.VMEM((groups, HD, near), BF16),
            pltpu.VMEM((groups, HD, near), BF16),
            pltpu.VMEM((near, HD), F32),
            pltpu.VMEM((near, HD), F32),
            [pltpu.VMEM((near, rows), F32)] * 3,
            [pltpu.VMEM((near, rows), F32)] * 3,
            [pltpu.VMEM((near, rows), BF16)] * 3,
            [pltpu.VMEM((near, rows), BF16)] * 2,
        ],
        compiler_params=params(),
        cost_estimate=cost(heads, rows, near, 6, 16),
        name="shared_pass",
    )(lengths, q, g, arrived, mixed, stats)


def run_own_backward(lengths, q, g, k, v, part, back):
    rows, width = q.shape
    heads, groups = width // HD, k.shape[1] // HD
    head, group, wide, stat = specs(rows, heads // groups)
    return pl.pallas_call(
        functools.partial(own_backward, per_group=heads // groups),
        grid=(heads // TURN,),
        in_specs=[
            pl.BlockSpec(memory_space=pltpu.SMEM), head, head, group, group, wide, stat
        ],
        out_specs=[head, group, group],
        out_shape=[shape((rows, width), BF16), shape(k.shape, BF16), shape(v.shape, BF16)],
        scratch_shapes=[
            pltpu.VMEM((HD, rows), BF16),
            pltpu.VMEM((rows, HD), F32),
            pltpu.VMEM((rows, HD), F32),
            [pltpu.VMEM((rows, rows), F32)] * 2,
            [pltpu.VMEM((rows, rows), F32)] * 2,
            [pltpu.VMEM((rows, rows), BF16)] * 2,
            [pltpu.VMEM((rows, rows), BF16)] * 2,
        ],
        compiler_params=params(),
        cost_estimate=cost(heads, rows, rows, 5, 12),
        name="own_backward",
    )(lengths, q, g, k, v, part, back)


def on_device(prompt_keys, prompt_values, q, resp_k, resp_v, grad_out, lengths):
    axes = ("prompt", "resp")
    shares = lax.axis_size("prompt")
    copies = lax.axis_size("resp")
    tokens, width = prompt_keys.shape
    chunk = 2 * tokens * width // shares // HD

    pieces = pl.pallas_call(
        copy_pieces,
        out_shape=shape((shares, copies, chunk, HD), BF16),
        compiler_params=pltpu.CompilerParams(vmem_limit_bytes=VMEM_LIMIT),
        name="copy_pieces",
    )(prompt_keys, prompt_values)
    pieces = pieces.reshape(shares * copies, chunk, HD)
    arrived = lax.all_to_all(pieces, axes, split_axis=0, concat_axis=0, tiled=True)

    mixed, stats = run_own_forward(q, resp_k, resp_v)
    attended, part, back, terms = run_shared(lengths, q, grad_out, arrived, mixed, stats)
    terms = lax.all_to_all(terms, axes, split_axis=0, concat_axis=0, tiled=True)
    query_grads, key_grads, value_grads = run_own_backward(
        lengths, q, grad_out, resp_k, resp_v, part, back
    )
    prompt_kg, prompt_vg = pl.pallas_call(
        add_terms,
        out_shape=[shape((tokens, width), BF16)] * 2,
        compiler_params=pltpu.CompilerParams(vmem_limit_bytes=VMEM_LIMIT),
        name="add_terms",
    )(terms.reshape(shares, copies, chunk, HD))
    return attended, query_grads, key_grads, value_grads, prompt_kg, prompt_vg


def solution(mesh):
    return jax.shard_map(
        on_device,
        mesh=mesh,
        in_specs=(
            P(("prompt", "resp"), None),
            P(("prompt", "resp"), None),
            P("resp", "prompt"),
            P("resp", "prompt"),
            P("resp", "prompt"),
            P("resp", "prompt"),
            P(),
        ),
        out_specs=(
            P("resp", "prompt"),
            P("resp", "prompt"),
            P("resp", "prompt"),
            P("resp", "prompt"),
            P(("prompt", "resp"), None),
            P(("prompt", "resp"), None),
        ),
        check_vma=False,
    )
```

```python
import functools
import math

import jax
import jax.numpy as jnp
from jax import lax
from jax.experimental import pallas as pl
from jax.experimental.pallas import tpu as pltpu
from jax.sharding import PartitionSpec as P

HD = 128
BLK = 256
SCALE = 1.0 / math.sqrt(HD)
EXP_SCALE = SCALE * math.log2(math.e)
NEG = -1e30
F32 = jnp.float32
BF16 = jnp.bfloat16


def dot_nt(a, b):
    return lax.dot_general(a, b, (((1,), (1,)), ((), ())), preferred_element_type=F32)


def dot_nn(a, b):
    return lax.dot_general(a, b, (((1,), (0,)), ((), ())), preferred_element_type=F32)


def live_rows(block, start, length):
    parts = []
    for at in range(0, block.shape[0], HD):
        factor = (start + at < length).astype(F32).astype(BF16)
        parts.append(block[at : at + HD] * factor)
    return jnp.concatenate(parts, axis=0)


def causal(s):
    key = lax.broadcasted_iota(jnp.int32, s.shape, 0)
    query = lax.broadcasted_iota(jnp.int32, s.shape, 1)
    return jnp.where(key <= query, s, NEG)


def stacked(ref, head):
    return ref[:, head * HD : (head + 1) * HD]


def own_forward(q_ref, k_ref, v_ref, mixed_ref, stats_ref, vt_ref, s_refs, w_refs, *, per_group):
    heads = mixed_ref.shape[0]
    rows = q_ref.shape[0]

    @pl.when(pl.program_id(0) % (per_group // heads) == 0)
    def _():
        vt_ref[...] = v_ref[...].T

    def scores(u):
        q = stacked(q_ref, u)
        for at in range(0, rows, BLK):
            end = at + BLK
            s_refs[u % 2][:end, at:end] = dot_nt(k_ref[:end, :], q[at:end])

    def mix(u):
        s_ref, w_ref = s_refs[u % 2], w_refs[u % 2]
        for at in range(0, rows, BLK):
            end = at + BLK
            tail = causal(s_ref[at:end, at:end])
            peak = jnp.max(tail, axis=0, keepdims=True)
            if at:
                peak = jnp.maximum(peak, jnp.max(s_ref[:at, at:end], axis=0, keepdims=True))
            e = jnp.exp2((tail - peak) * EXP_SCALE)
            total = jnp.sum(e, axis=0, keepdims=True)
            w_ref[at:end, at:end] = e.astype(BF16)
            if at:
                e = jnp.exp2((s_ref[:at, at:end] - peak) * EXP_SCALE)
                total += jnp.sum(e, axis=0, keepdims=True)
                w_ref[:at, at:end] = e.astype(BF16)
            mixed_ref[u, :, at:end] = dot_nn(vt_ref[:, :end], w_ref[:end, at:end])
            stats_ref[u, 0:1, at:end] = peak
            stats_ref[u, 1:2, at:end] = total

    for step in range(heads + 1):
        if step < heads:
            scores(step)
        if step:
            mix(step - 1)


def shared_pass(
    lengths_ref, q_ref, g_ref, near_ref, mixed_ref, stats_ref,
    att_ref, qg_ref, back_ref, terms_ref,
    near_wide, k_ref, v_ref, kt_ref, vt_ref, kg_ref, vg_ref, s_refs, dp_refs, w_refs, ds_refs,
    *, per_group
):
    length = lengths_ref[lax.axis_index("resp")]
    heads = mixed_ref.shape[0]
    rows = q_ref.shape[0]
    groups, near = k_ref.shape[:2]
    senders, chunk = near_ref.shape[:2]
    tokens = near // senders
    steps = per_group // heads
    step_id = pl.program_id(0)
    group = step_id // steps

    @pl.when(step_id == 0)
    def _():
        near_wide[...] = near_ref[...].astype(F32).reshape(senders * chunk, HD)
        for which, (ref, t_ref) in enumerate(((k_ref, kt_ref), (v_ref, vt_ref))):
            for one in range(groups):
                for token in range(tokens):
                    row = (which * groups + one) * tokens + token
                    piece = near_wide[pl.ds(row, senders, stride=chunk), :].astype(BF16)
                    ref[one, token * senders : (token + 1) * senders, :] = piece
                t_ref[one] = ref[one].T

    @pl.when(step_id % steps == 0)
    def _():
        kg_ref[...] = jnp.zeros_like(kg_ref)
        vg_ref[...] = jnp.zeros_like(vg_ref)

    peaks, inverses, drifts, scaled = {}, {}, {}, {}

    def grads(u):
        return live_rows(stacked(g_ref, u), 0, length)

    def scores(u):
        s = dot_nt(k_ref[group], stacked(q_ref, u))
        s_refs[u % 3][...] = s
        peaks[u] = jnp.maximum(jnp.max(s, axis=0, keepdims=True), stats_ref[u, 0:1, :])
        dp_refs[u % 3][...] = dot_nt(v_ref[group], grads(u))

    def mix(u):
        s_ref, w_ref = s_refs[u % 3], w_refs[u % 3]
        e = jnp.exp2((s_ref[...] - peaks[u]) * EXP_SCALE)
        s_ref[...] = e
        decay = jnp.exp2((stats_ref[u, 0:1, :] - peaks[u]) * EXP_SCALE)
        total = jnp.sum(e, axis=0, keepdims=True) + stats_ref[u, 1:2, :] * decay
        inverses[u] = 1.0 / total
        w_ref[...] = (s_ref[...] * inverses[u]).astype(BF16)
        mixed = dot_nn(vt_ref[group], w_ref[...]) + mixed_ref[u] * (decay * inverses[u])
        live = lax.broadcasted_iota(jnp.int32, (1, rows), 1) < length
        att_ref[:, u * HD : (u + 1) * HD] = jnp.where(live, mixed, 0.0).T.astype(BF16)
        drifts[u] = jnp.sum(grads(u).T.astype(F32) * mixed, axis=0, keepdims=True)
        back_ref[u, 0:1, :] = peaks[u]
        back_ref[u, 1:2, :] = inverses[u]
        back_ref[u, 2:3, :] = drifts[u]

    def spread(u):
        s_ref, dp_ref, w_ref, ds_ref = s_refs[u % 3], dp_refs[u % 3], w_refs[u % 3], ds_refs[u % 2]
        ds = s_ref[...] * (dp_ref[...] - drifts[u]) * (inverses[u] * SCALE)
        ds_ref[...] = ds.astype(BF16)
        qg_ref[u] = dot_nn(kt_ref[group], ds_ref[...])
        kg_ref[...] += dot_nn(ds_ref[...], stacked(q_ref, u))
        vg_ref[...] += dot_nn(w_ref[...], grads(u))

    for step in range(heads + 2):
        if step < heads:
            scores(step)
        if 0 <= step - 1 < heads:
            mix(step - 1)
        if step >= 2:
            spread(step - 2)

    for one in range(groups):
        @pl.when(step_id == (one + 1) * steps - 1)
        def _():
            for which, ref in enumerate((kg_ref, vg_ref)):
                for token in range(tokens):
                    row = (which * groups + one) * tokens + token
                    near_wide[pl.ds(row, senders, stride=chunk), :] = ref[
                        token * senders : (token + 1) * senders, :
                    ]

    @pl.when(step_id == groups * steps - 1)
    def _():
        terms_ref[...] = near_wide[...].reshape(senders, chunk, HD).astype(BF16)


def own_backward(
    lengths_ref, q_ref, g_ref, k_ref, v_ref, part_ref, back_ref,
    qg_ref, kg_ref, vg_ref, kt_ref, kacc_ref, vacc_ref, s_refs, dp_refs, w_refs, ds_refs,
    *, per_group
):
    length = lengths_ref[lax.axis_index("resp")]
    heads = part_ref.shape[0]
    rows = q_ref.shape[0]
    steps = per_group // heads
    turn = pl.program_id(0) % steps

    @pl.when(turn == 0)
    def _():
        kt_ref[...] = k_ref[...].T
        kacc_ref[...] = jnp.zeros_like(kacc_ref)
        vacc_ref[...] = jnp.zeros_like(vacc_ref)

    def scores(u):
        q = stacked(q_ref, u)
        g = live_rows(stacked(g_ref, u), 0, length)
        for at in range(0, rows, BLK):
            end = at + BLK
            s_refs[u % 2][:end, at:end] = dot_nt(k_ref[:end, :], q[at:end])
            dp_refs[u % 2][:end, at:end] = dot_nt(v_ref[:end, :], g[at:end])

    def spread(u):
        s_ref, dp_ref, w_ref, ds_ref = (refs[u % 2] for refs in (s_refs, dp_refs, w_refs, ds_refs))
        q = stacked(q_ref, u)
        g = live_rows(stacked(g_ref, u), 0, length)
        for at in range(0, rows, BLK):
            end = at + BLK
            peak = back_ref[u, 0:1, at:end]
            inverse = back_ref[u, 1:2, at:end]
            drift = back_ref[u, 2:3, at:end]
            for low in range(0, end, BLK):
                keys = slice(low, low + BLK)
                s = s_ref[keys, at:end]
                if low == at:
                    s = causal(s)
                p = jnp.exp2((s - peak) * EXP_SCALE) * inverse
                w_ref[keys, at:end] = p.astype(BF16)
                ds_ref[keys, at:end] = (p * (dp_ref[keys, at:end] - drift) * SCALE).astype(BF16)
            qg = dot_nn(kt_ref[:, :end], ds_ref[:end, at:end]) + part_ref[u, :, at:end]
            qg_ref[at:end, u * HD : (u + 1) * HD] = qg.T.astype(BF16)
        for low in range(0, rows, BLK):
            keys = slice(low, low + BLK)
            kacc_ref[keys, :] += dot_nn(ds_ref[keys, low:], q[low:])
            vacc_ref[keys, :] += dot_nn(w_ref[keys, low:], g[low:])

    for step in range(heads + 1):
        if step < heads:
            scores(step)
        if step:
            spread(step - 1)

    @pl.when(turn == steps - 1)
    def _():
        kg_ref[...] = kacc_ref[...].astype(BF16)
        vg_ref[...] = vacc_ref[...].astype(BF16)


def copy_pieces(k_ref, v_ref, out_ref):
    tokens, width = k_ref.shape
    shares, copies = out_ref.shape[:2]
    groups = width // shares // HD
    for share in range(shares):
        parts = []
        for ref in (k_ref, v_ref):
            for one in range(groups):
                at = (share * groups + one) * HD
                parts.append(ref[:, at : at + HD].astype(F32))
        piece = jnp.concatenate(parts, axis=0).astype(BF16)
        out_ref[share] = jnp.broadcast_to(piece[None], (copies,) + piece.shape)


def add_terms(terms_ref, k_ref, v_ref):
    tokens, width = k_ref.shape
    shares = terms_ref.shape[0]
    groups = width // shares // HD
    for share in range(shares):
        total = jnp.sum(terms_ref[share].astype(F32), axis=0)
        for which, ref in enumerate((k_ref, v_ref)):
            for one in range(groups):
                row = (which * groups + one) * tokens
                at = (share * groups + one) * HD
                ref[:, at : at + HD] = total[row : row + tokens].astype(BF16)


VMEM_LIMIT = 40 * 2**20
TURN = 4


def params():
    return pltpu.CompilerParams(
        dimension_semantics=("arbitrary",), vmem_limit_bytes=VMEM_LIMIT
    )


def shape(dims, dtype=F32):
    return jax.ShapeDtypeStruct(dims, dtype)


def hbm_shape(dims, dtype=F32):
    return pltpu.HBM(dims, dtype)


def in_hbm(*arrays):
    return tuple(pltpu.with_memory_space_constraint(a, pltpu.HBM) for a in arrays)


def specs(rows, per_group):
    steps = per_group // TURN
    return (
        pl.BlockSpec((rows, TURN * HD), lambda h: (0, h)),
        pl.BlockSpec((rows, HD), lambda h: (0, h // steps)),
        pl.BlockSpec((TURN, HD, rows), lambda h: (h, 0, 0)),
        pl.BlockSpec((TURN, 8, rows), lambda h: (h, 0, 0)),
    )


def cost(heads, rows, keys, matmuls, mib):
    return pl.CostEstimate(
        flops=2 * matmuls * heads * rows * keys * HD,
        bytes_accessed=mib * 2**20,
        transcendentals=heads * rows * keys,
    )


def run_own_forward(q, k, v):
    rows, width = q.shape
    heads, groups = width // HD, k.shape[1] // HD
    head, group, wide, stat = specs(rows, heads // groups)
    return pl.pallas_call(
        functools.partial(own_forward, per_group=heads // groups),
        grid=(heads // TURN,),
        in_specs=[head, group, group],
        out_specs=[wide, stat],
        out_shape=[hbm_shape((heads, HD, rows)), hbm_shape((heads, 8, rows))],
        scratch_shapes=[
            pltpu.VMEM((HD, rows), BF16),
            [pltpu.VMEM((rows, rows), F32)] * 2,
            [pltpu.VMEM((rows, rows), BF16)] * 2,
        ],
        compiler_params=params(),
        cost_estimate=cost(heads, rows, rows, 2, 8),
        name="own_forward",
    )(q, k, v)


def run_shared(lengths, q, g, arrived, mixed, stats):
    rows, width = q.shape
    heads = width // HD
    senders, chunk = arrived.shape[:2]
    groups = 2
    near = senders * chunk // (2 * groups)
    head, _, wide, stat = specs(rows, heads // groups)
    whole = pl.BlockSpec(arrived.shape, lambda h: (0, 0, 0))
    return pl.pallas_call(
        functools.partial(shared_pass, per_group=heads // groups),
        grid=(heads // TURN,),
        in_specs=[pl.BlockSpec(memory_space=pltpu.SMEM), head, head, whole, wide, stat],
        out_specs=[head, wide, stat, whole],
        out_shape=[
            hbm_shape((rows, width), BF16), hbm_shape((heads, HD, rows)),
            hbm_shape((heads, 8, rows)), hbm_shape(arrived.shape, BF16),
        ],
        scratch_shapes=[
            pltpu.VMEM((senders * chunk, HD), F32),
            pltpu.VMEM((groups, near, HD), BF16),
            pltpu.VMEM((groups, near, HD), BF16),
            pltpu.VMEM((groups, HD, near), BF16),
            pltpu.VMEM((groups, HD, near), BF16),
            pltpu.VMEM((near, HD), F32),
            pltpu.VMEM((near, HD), F32),
            [pltpu.VMEM((near, rows), F32)] * 3,
            [pltpu.VMEM((near, rows), F32)] * 3,
            [pltpu.VMEM((near, rows), BF16)] * 3,
            [pltpu.VMEM((near, rows), BF16)] * 2,
        ],
        compiler_params=params(),
        cost_estimate=cost(heads, rows, near, 6, 16),
        name="shared_pass",
    )(lengths, q, g, arrived, mixed, stats)


def run_own_backward(lengths, q, g, k, v, part, back):
    rows, width = q.shape
    heads, groups = width // HD, k.shape[1] // HD
    head, group, wide, stat = specs(rows, heads // groups)
    return pl.pallas_call(
        functools.partial(own_backward, per_group=heads // groups),
        grid=(heads // TURN,),
        in_specs=[
            pl.BlockSpec(memory_space=pltpu.SMEM), head, head, group, group, wide, stat
        ],
        out_specs=[head, group, group],
        out_shape=[shape((rows, width), BF16), shape(k.shape, BF16), shape(v.shape, BF16)],
        scratch_shapes=[
            pltpu.VMEM((HD, rows), BF16),
            pltpu.VMEM((rows, HD), F32),
            pltpu.VMEM((rows, HD), F32),
            [pltpu.VMEM((rows, rows), F32)] * 2,
            [pltpu.VMEM((rows, rows), F32)] * 2,
            [pltpu.VMEM((rows, rows), BF16)] * 2,
            [pltpu.VMEM((rows, rows), BF16)] * 2,
        ],
        compiler_params=params(),
        cost_estimate=cost(heads, rows, rows, 5, 12),
        name="own_backward",
    )(lengths, q, g, k, v, part, back)


def on_device(prompt_keys, prompt_values, q, resp_k, resp_v, grad_out, lengths):
    axes = ("prompt", "resp")
    shares = lax.axis_size("prompt")
    copies = lax.axis_size("resp")
    tokens, width = prompt_keys.shape
    chunk = 2 * tokens * width // shares // HD

    prompt_keys, prompt_values = in_hbm(prompt_keys, prompt_values)
    pieces = pl.pallas_call(
        copy_pieces,
        out_shape=shape((shares, copies, chunk, HD), BF16),
        compiler_params=pltpu.CompilerParams(vmem_limit_bytes=VMEM_LIMIT),
        name="copy_pieces",
    )(prompt_keys, prompt_values)
    pieces = pieces.reshape(shares * copies, chunk, HD)
    arrived = lax.all_to_all(pieces, axes, split_axis=0, concat_axis=0, tiled=True)

    q, resp_k, resp_v, grad_out = in_hbm(q, resp_k, resp_v, grad_out)
    mixed, stats = in_hbm(*run_own_forward(q, resp_k, resp_v))
    attended, part, back, terms = run_shared(lengths, q, grad_out, arrived, mixed, stats)
    part, back = in_hbm(part, back)
    terms = lax.all_to_all(terms, axes, split_axis=0, concat_axis=0, tiled=True)
    query_grads, key_grads, value_grads = run_own_backward(
        lengths, q, grad_out, resp_k, resp_v, part, back
    )
    prompt_kg, prompt_vg = pl.pallas_call(
        add_terms,
        out_shape=[shape((tokens, width), BF16)] * 2,
        compiler_params=pltpu.CompilerParams(vmem_limit_bytes=VMEM_LIMIT),
        name="add_terms",
    )(terms.reshape(shares, copies, chunk, HD))
    return attended, query_grads, key_grads, value_grads, prompt_kg, prompt_vg


def solution(mesh):
    return jax.shard_map(
        on_device,
        mesh=mesh,
        in_specs=(
            P(("prompt", "resp"), None),
            P(("prompt", "resp"), None),
            P("resp", "prompt"),
            P("resp", "prompt"),
            P("resp", "prompt"),
            P("resp", "prompt"),
            P(),
        ),
        out_specs=(
            P("resp", "prompt"),
            P("resp", "prompt"),
            P("resp", "prompt"),
            P("resp", "prompt"),
            P(("prompt", "resp"), None),
            P(("prompt", "resp"), None),
        ),
        check_vma=False,
    )
```

```python
import functools
import math

import jax
import jax.numpy as jnp
from jax import lax
from jax.experimental import pallas as pl
from jax.experimental.pallas import tpu as pltpu
from jax.sharding import PartitionSpec as P

HD = 128
BLK = 256
SCALE = 1.0 / math.sqrt(HD)
EXP_SCALE = SCALE * math.log2(math.e)
NEG = -1e30
REACH = 100 / EXP_SCALE
SLACK = 1.02
F32 = jnp.float32
BF16 = jnp.bfloat16


def dot_nt(a, b):
    return lax.dot_general(a, b, (((1,), (1,)), ((), ())), preferred_element_type=F32)


def dot_nn(a, b):
    return lax.dot_general(a, b, (((1,), (0,)), ((), ())), preferred_element_type=F32)


def live_rows(block, start, length):
    parts = []
    for at in range(0, block.shape[0], HD):
        factor = (start + at < length).astype(F32).astype(BF16)
        parts.append(block[at : at + HD] * factor)
    return jnp.concatenate(parts, axis=0)


def causal(s):
    key = lax.broadcasted_iota(jnp.int32, s.shape, 0)
    query = lax.broadcasted_iota(jnp.int32, s.shape, 1)
    return jnp.where(key <= query, s, NEG)


def stacked(ref, head):
    return ref[:, head * HD : (head + 1) * HD]


def own_forward(
    q_ref, k_ref, v_ref, mixed_ref, stats_ref, limit_ref, vt_ref, s_refs, w_refs, *, per_group
):
    heads = mixed_ref.shape[0]
    rows = q_ref.shape[0]

    @pl.when(pl.program_id(0) % (per_group // heads) == 0)
    def _():
        vt_ref[...] = v_ref[...].T

    @pl.when(pl.program_id(0) == 0)
    def _():
        limit_ref[...] = jnp.full(limit_ref.shape, NEG, F32)

    def scores(u):
        q = stacked(q_ref, u)
        for at in range(0, rows, BLK):
            end = at + BLK
            s_refs[u % 2][:end, at:end] = dot_nt(k_ref[:end, :], q[at:end])
        square = dot_nt(jnp.ones((8, HD), BF16), q * q)
        limit_ref[0:8, :] = jnp.maximum(limit_ref[0:8, :], square)

    def mix(u):
        s_ref, w_ref = s_refs[u % 2], w_refs[u % 2]
        for at in range(0, rows, BLK):
            end = at + BLK
            tail = causal(s_ref[at:end, at:end])
            peak = jnp.max(tail, axis=0, keepdims=True)
            if at:
                peak = jnp.maximum(peak, jnp.max(s_ref[:at, at:end], axis=0, keepdims=True))
            e = jnp.exp2((tail - peak) * EXP_SCALE)
            total = jnp.sum(e, axis=0, keepdims=True)
            w_ref[at:end, at:end] = e.astype(BF16)
            if at:
                e = jnp.exp2((s_ref[:at, at:end] - peak) * EXP_SCALE)
                total += jnp.sum(e, axis=0, keepdims=True)
                w_ref[:at, at:end] = e.astype(BF16)
            mixed_ref[u, :, at:end] = dot_nn(vt_ref[:, :end], w_ref[:end, at:end])
            stats_ref[u, 0:1, at:end] = peak
            stats_ref[u, 1:2, at:end] = total
            limit_ref[8:9, at:end] = jnp.maximum(limit_ref[8:9, at:end], -peak)

    for step in range(heads + 1):
        if step < heads:
            scores(step)
        if step:
            mix(step - 1)


def shared_pass(
    lengths_ref, q_ref, g_ref, near_ref, mixed_ref, stats_ref, limit_ref,
    att_ref, qg_ref, back_ref, terms_ref,
    near_wide, k_ref, v_ref, kt_ref, vt_ref, kg_ref, vg_ref, s_refs, dp_refs, w_refs, ds_refs,
    peak_ref, close_ref,
    *, per_group
):
    length = lengths_ref[lax.axis_index("resp")]
    heads = mixed_ref.shape[0]
    rows = q_ref.shape[0]
    groups, near = k_ref.shape[:2]
    senders, chunk = near_ref.shape[:2]
    tokens = near // senders
    steps = per_group // heads
    step_id = pl.program_id(0)
    group = step_id // steps

    @pl.when(step_id == 0)
    def _():
        near_wide[...] = near_ref[...].astype(F32).reshape(senders * chunk, HD)
        for which, (ref, t_ref) in enumerate(((k_ref, kt_ref), (v_ref, vt_ref))):
            for one in range(groups):
                for token in range(tokens):
                    row = (which * groups + one) * tokens + token
                    piece = near_wide[pl.ds(row, senders, stride=chunk), :].astype(BF16)
                    ref[one, token * senders : (token + 1) * senders, :] = piece
                t_ref[one] = ref[one].T
        wide = kt_ref[...].astype(F32)
        longest = jnp.sqrt(jnp.max(jnp.sum(wide * wide, axis=1)) * jnp.max(limit_ref[0:8, :]))
        close_ref[0] = (longest * SLACK + jnp.max(limit_ref[8:9, :]) < REACH).astype(jnp.int32)

    @pl.when(step_id % steps == 0)
    def _():
        kg_ref[...] = jnp.zeros_like(kg_ref)
        vg_ref[...] = jnp.zeros_like(vg_ref)

    @pl.when(close_ref[0] != 0)
    def _():
        for u in range(heads):
            peak_ref[u, 0:1, :] = stats_ref[u, 0:1, :]

    @pl.when(close_ref[0] == 0)
    def _():
        for u in range(heads):
            s = dot_nt(k_ref[group], stacked(q_ref, u))
            peak = jnp.max(s, axis=0, keepdims=True)
            peak_ref[u, 0:1, :] = jnp.maximum(peak, stats_ref[u, 0:1, :])

    inverses, drifts = {}, {}

    def grads(u):
        return live_rows(stacked(g_ref, u), 0, length)

    def scores(u):
        s_refs[u % 3][...] = dot_nt(k_ref[group], stacked(q_ref, u))
        dp_refs[u % 3][...] = dot_nt(v_ref[group], grads(u))

    def mix(u):
        s_ref, w_ref = s_refs[u % 3], w_refs[u % 3]
        peak = peak_ref[u, 0:1, :]
        e = jnp.exp2((s_ref[...] - peak) * EXP_SCALE)
        s_ref[...] = e
        decay = jnp.exp2((stats_ref[u, 0:1, :] - peak) * EXP_SCALE)
        total = jnp.sum(e, axis=0, keepdims=True) + stats_ref[u, 1:2, :] * decay
        inverses[u] = 1.0 / total
        w_ref[...] = (s_ref[...] * inverses[u]).astype(BF16)
        mixed = dot_nn(vt_ref[group], w_ref[...]) + mixed_ref[u] * (decay * inverses[u])
        live = lax.broadcasted_iota(jnp.int32, (1, rows), 1) < length
        att_ref[:, u * HD : (u + 1) * HD] = jnp.where(live, mixed, 0.0).T.astype(BF16)
        drifts[u] = jnp.sum(grads(u).T.astype(F32) * mixed, axis=0, keepdims=True)
        back_ref[u, 0:1, :] = peak
        back_ref[u, 1:2, :] = inverses[u]
        back_ref[u, 2:3, :] = drifts[u]

    def spread(u):
        s_ref, dp_ref, w_ref, ds_ref = s_refs[u % 3], dp_refs[u % 3], w_refs[u % 3], ds_refs[u % 2]
        ds = s_ref[...] * (dp_ref[...] - drifts[u]) * (inverses[u] * SCALE)
        ds_ref[...] = ds.astype(BF16)
        qg_ref[u] = dot_nn(kt_ref[group], ds_ref[...])
        kg_ref[...] += dot_nn(ds_ref[...], stacked(q_ref, u))
        vg_ref[...] += dot_nn(w_ref[...], grads(u))

    for step in range(heads + 2):
        if step < heads:
            scores(step)
        if 0 <= step - 1 < heads:
            mix(step - 1)
        if step >= 2:
            spread(step - 2)

    for one in range(groups):
        @pl.when(step_id == (one + 1) * steps - 1)
        def _():
            for which, ref in enumerate((kg_ref, vg_ref)):
                for token in range(tokens):
                    row = (which * groups + one) * tokens + token
                    near_wide[pl.ds(row, senders, stride=chunk), :] = ref[
                        token * senders : (token + 1) * senders, :
                    ]

    @pl.when(step_id == groups * steps - 1)
    def _():
        terms_ref[...] = near_wide[...].reshape(senders, chunk, HD).astype(BF16)


def own_backward(
    lengths_ref, q_ref, g_ref, k_ref, v_ref, part_ref, back_ref,
    qg_ref, kg_ref, vg_ref, kt_ref, kacc_ref, vacc_ref, s_refs, dp_refs, w_refs, ds_refs,
    *, per_group
):
    length = lengths_ref[lax.axis_index("resp")]
    heads = part_ref.shape[0]
    rows = q_ref.shape[0]
    steps = per_group // heads
    turn = pl.program_id(0) % steps

    @pl.when(turn == 0)
    def _():
        kt_ref[...] = k_ref[...].T
        kacc_ref[...] = jnp.zeros_like(kacc_ref)
        vacc_ref[...] = jnp.zeros_like(vacc_ref)

    def scores(u):
        q = stacked(q_ref, u)
        g = live_rows(stacked(g_ref, u), 0, length)
        for at in range(0, rows, BLK):
            end = at + BLK
            s_refs[u % 2][:end, at:end] = dot_nt(k_ref[:end, :], q[at:end])
            dp_refs[u % 2][:end, at:end] = dot_nt(v_ref[:end, :], g[at:end])

    def spread(u):
        s_ref, dp_ref, w_ref, ds_ref = (refs[u % 2] for refs in (s_refs, dp_refs, w_refs, ds_refs))
        q = stacked(q_ref, u)
        g = live_rows(stacked(g_ref, u), 0, length)
        for at in range(0, rows, BLK):
            end = at + BLK
            peak = back_ref[u, 0:1, at:end]
            inverse = back_ref[u, 1:2, at:end]
            drift = back_ref[u, 2:3, at:end]
            for low in range(0, end, BLK):
                keys = slice(low, low + BLK)
                s = s_ref[keys, at:end]
                if low == at:
                    s = causal(s)
                p = jnp.exp2((s - peak) * EXP_SCALE) * inverse
                w_ref[keys, at:end] = p.astype(BF16)
                ds_ref[keys, at:end] = (p * (dp_ref[keys, at:end] - drift) * SCALE).astype(BF16)
            qg = dot_nn(kt_ref[:, :end], ds_ref[:end, at:end]) + part_ref[u, :, at:end]
            qg_ref[at:end, u * HD : (u + 1) * HD] = qg.T.astype(BF16)
        for low in range(0, rows, BLK):
            keys = slice(low, low + BLK)
            kacc_ref[keys, :] += dot_nn(ds_ref[keys, low:], q[low:])
            vacc_ref[keys, :] += dot_nn(w_ref[keys, low:], g[low:])

    for step in range(heads + 1):
        if step < heads:
            scores(step)
        if step:
            spread(step - 1)

    @pl.when(turn == steps - 1)
    def _():
        kg_ref[...] = kacc_ref[...].astype(BF16)
        vg_ref[...] = vacc_ref[...].astype(BF16)


def copy_pieces(k_ref, v_ref, out_ref):
    tokens, width = k_ref.shape
    shares, copies = out_ref.shape[:2]
    groups = width // shares // HD
    for share in range(shares):
        parts = []
        for ref in (k_ref, v_ref):
            for one in range(groups):
                at = (share * groups + one) * HD
                parts.append(ref[:, at : at + HD].astype(F32))
        piece = jnp.concatenate(parts, axis=0).astype(BF16)
        out_ref[share] = jnp.broadcast_to(piece[None], (copies,) + piece.shape)


def add_terms(terms_ref, k_ref, v_ref):
    tokens, width = k_ref.shape
    shares = terms_ref.shape[0]
    groups = width // shares // HD
    for share in range(shares):
        total = jnp.sum(terms_ref[share].astype(F32), axis=0)
        for which, ref in enumerate((k_ref, v_ref)):
            for one in range(groups):
                row = (which * groups + one) * tokens
                at = (share * groups + one) * HD
                ref[:, at : at + HD] = total[row : row + tokens].astype(BF16)


VMEM_LIMIT = 40 * 2**20
TURN = 4


def params():
    return pltpu.CompilerParams(
        dimension_semantics=("arbitrary",), vmem_limit_bytes=VMEM_LIMIT
    )


def shape(dims, dtype=F32):
    return jax.ShapeDtypeStruct(dims, dtype)


def hbm_shape(dims, dtype=F32):
    return pltpu.HBM(dims, dtype)


def in_hbm(*arrays):
    return tuple(pltpu.with_memory_space_constraint(a, pltpu.HBM) for a in arrays)


def specs(rows, per_group):
    steps = per_group // TURN
    return (
        pl.BlockSpec((rows, TURN * HD), lambda h: (0, h)),
        pl.BlockSpec((rows, HD), lambda h: (0, h // steps)),
        pl.BlockSpec((TURN, HD, rows), lambda h: (h, 0, 0)),
        pl.BlockSpec((TURN, 8, rows), lambda h: (h, 0, 0)),
    )


def cost(heads, rows, keys, matmuls, mib):
    return pl.CostEstimate(
        flops=2 * matmuls * heads * rows * keys * HD,
        bytes_accessed=mib * 2**20,
        transcendentals=heads * rows * keys,
    )


def run_own_forward(q, k, v):
    rows, width = q.shape
    heads, groups = width // HD, k.shape[1] // HD
    head, group, wide, stat = specs(rows, heads // groups)
    return pl.pallas_call(
        functools.partial(own_forward, per_group=heads // groups),
        grid=(heads // TURN,),
        in_specs=[head, group, group],
        out_specs=[wide, stat, pl.BlockSpec((16, rows), lambda h: (0, 0))],
        out_shape=[
            hbm_shape((heads, HD, rows)), hbm_shape((heads, 8, rows)), hbm_shape((16, rows)),
        ],
        scratch_shapes=[
            pltpu.VMEM((HD, rows), BF16),
            [pltpu.VMEM((rows, rows), F32)] * 2,
            [pltpu.VMEM((rows, rows), BF16)] * 2,
        ],
        compiler_params=params(),
        cost_estimate=cost(heads, rows, rows, 2, 8),
        name="own_forward",
    )(q, k, v)


def run_shared(lengths, q, g, arrived, mixed, stats, limit):
    rows, width = q.shape
    heads = width // HD
    senders, chunk = arrived.shape[:2]
    groups = 2
    near = senders * chunk // (2 * groups)
    head, _, wide, stat = specs(rows, heads // groups)
    whole = pl.BlockSpec(arrived.shape, lambda h: (0, 0, 0))
    return pl.pallas_call(
        functools.partial(shared_pass, per_group=heads // groups),
        grid=(heads // TURN,),
        in_specs=[
            pl.BlockSpec(memory_space=pltpu.SMEM), head, head, whole, wide, stat,
            pl.BlockSpec((16, rows), lambda h: (0, 0)),
        ],
        out_specs=[head, wide, stat, whole],
        out_shape=[
            hbm_shape((rows, width), BF16), hbm_shape((heads, HD, rows)),
            hbm_shape((heads, 8, rows)), hbm_shape(arrived.shape, BF16),
        ],
        scratch_shapes=[
            pltpu.VMEM((senders * chunk, HD), F32),
            pltpu.VMEM((groups, near, HD), BF16),
            pltpu.VMEM((groups, near, HD), BF16),
            pltpu.VMEM((groups, HD, near), BF16),
            pltpu.VMEM((groups, HD, near), BF16),
            pltpu.VMEM((near, HD), F32),
            pltpu.VMEM((near, HD), F32),
            [pltpu.VMEM((near, rows), F32)] * 3,
            [pltpu.VMEM((near, rows), F32)] * 3,
            [pltpu.VMEM((near, rows), BF16)] * 3,
            [pltpu.VMEM((near, rows), BF16)] * 2,
            pltpu.VMEM((TURN, 8, rows), F32),
            pltpu.SMEM((1,), jnp.int32),
        ],
        compiler_params=params(),
        cost_estimate=cost(heads, rows, near, 6, 16),
        name="shared_pass",
    )(lengths, q, g, arrived, mixed, stats, limit)


def run_own_backward(lengths, q, g, k, v, part, back):
    rows, width = q.shape
    heads, groups = width // HD, k.shape[1] // HD
    head, group, wide, stat = specs(rows, heads // groups)
    return pl.pallas_call(
        functools.partial(own_backward, per_group=heads // groups),
        grid=(heads // TURN,),
        in_specs=[
            pl.BlockSpec(memory_space=pltpu.SMEM), head, head, group, group, wide, stat
        ],
        out_specs=[head, group, group],
        out_shape=[shape((rows, width), BF16), shape(k.shape, BF16), shape(v.shape, BF16)],
        scratch_shapes=[
            pltpu.VMEM((HD, rows), BF16),
            pltpu.VMEM((rows, HD), F32),
            pltpu.VMEM((rows, HD), F32),
            [pltpu.VMEM((rows, rows), F32)] * 2,
            [pltpu.VMEM((rows, rows), F32)] * 2,
            [pltpu.VMEM((rows, rows), BF16)] * 2,
            [pltpu.VMEM((rows, rows), BF16)] * 2,
        ],
        compiler_params=params(),
        cost_estimate=cost(heads, rows, rows, 5, 12),
        name="own_backward",
    )(lengths, q, g, k, v, part, back)


def on_device(prompt_keys, prompt_values, q, resp_k, resp_v, grad_out, lengths):
    axes = ("prompt", "resp")
    shares = lax.axis_size("prompt")
    copies = lax.axis_size("resp")
    tokens, width = prompt_keys.shape
    chunk = 2 * tokens * width // shares // HD

    prompt_keys, prompt_values = in_hbm(prompt_keys, prompt_values)
    pieces = pl.pallas_call(
        copy_pieces,
        out_shape=shape((shares, copies, chunk, HD), BF16),
        compiler_params=pltpu.CompilerParams(vmem_limit_bytes=VMEM_LIMIT),
        name="copy_pieces",
    )(prompt_keys, prompt_values)
    pieces = pieces.reshape(shares * copies, chunk, HD)
    arrived = lax.all_to_all(pieces, axes, split_axis=0, concat_axis=0, tiled=True)

    q, resp_k, resp_v, grad_out = in_hbm(q, resp_k, resp_v, grad_out)
    mixed, stats, limit = in_hbm(*run_own_forward(q, resp_k, resp_v))
    attended, part, back, terms = run_shared(
        lengths, q, grad_out, arrived, mixed, stats, limit
    )
    part, back = in_hbm(part, back)
    terms = lax.all_to_all(terms, axes, split_axis=0, concat_axis=0, tiled=True)
    query_grads, key_grads, value_grads = run_own_backward(
        lengths, q, grad_out, resp_k, resp_v, part, back
    )
    prompt_kg, prompt_vg = pl.pallas_call(
        add_terms,
        out_shape=[shape((tokens, width), BF16)] * 2,
        compiler_params=pltpu.CompilerParams(vmem_limit_bytes=VMEM_LIMIT),
        name="add_terms",
    )(terms.reshape(shares, copies, chunk, HD))
    return attended, query_grads, key_grads, value_grads, prompt_kg, prompt_vg


def solution(mesh):
    return jax.shard_map(
        on_device,
        mesh=mesh,
        in_specs=(
            P(("prompt", "resp"), None),
            P(("prompt", "resp"), None),
            P("resp", "prompt"),
            P("resp", "prompt"),
            P("resp", "prompt"),
            P("resp", "prompt"),
            P(),
        ),
        out_specs=(
            P("resp", "prompt"),
            P("resp", "prompt"),
            P("resp", "prompt"),
            P("resp", "prompt"),
            P(("prompt", "resp"), None),
            P(("prompt", "resp"), None),
        ),
        check_vma=False,
    )
```

```python
import functools
import math

import jax
import jax.numpy as jnp
from jax import lax
from jax.experimental import pallas as pl
from jax.experimental.pallas import tpu as pltpu
from jax.sharding import PartitionSpec as P

HD = 128
BLK = 256
SCALE = 1.0 / math.sqrt(HD)
EXP_SCALE = SCALE * math.log2(math.e)
NEG = -1e30
REACH = 100 / EXP_SCALE
SLACK = 1.02
F32 = jnp.float32
BF16 = jnp.bfloat16


def dot_nt(a, b):
    return lax.dot_general(a, b, (((1,), (1,)), ((), ())), preferred_element_type=F32)


def dot_nn(a, b):
    return lax.dot_general(a, b, (((1,), (0,)), ((), ())), preferred_element_type=F32)


def live_rows(block, start, length):
    parts = []
    for at in range(0, block.shape[0], HD):
        factor = (start + at < length).astype(F32).astype(BF16)
        parts.append(block[at : at + HD] * factor)
    return jnp.concatenate(parts, axis=0)


def causal(s):
    key = lax.broadcasted_iota(jnp.int32, s.shape, 0)
    query = lax.broadcasted_iota(jnp.int32, s.shape, 1)
    return jnp.where(key <= query, s, NEG)


def stacked(ref, head):
    return ref[:, head * HD : (head + 1) * HD]


def own_forward(
    q_ref, k_ref, v_ref, mixed_ref, stats_ref, limit_ref, vt_ref, s_refs, w_refs, *, per_group
):
    heads = mixed_ref.shape[0]
    rows = q_ref.shape[0]

    @pl.when(pl.program_id(0) % (per_group // heads) == 0)
    def _():
        vt_ref[...] = v_ref[...].T

    @pl.when(pl.program_id(0) == 0)
    def _():
        limit_ref[...] = jnp.full(limit_ref.shape, NEG, F32)

    def scores(u):
        q = stacked(q_ref, u)
        for at in range(0, rows, BLK):
            end = at + BLK
            s_refs[u % 2][:end, at:end] = dot_nt(k_ref[:end, :], q[at:end])
        square = dot_nt(jnp.ones((8, HD), BF16), q * q)
        limit_ref[0:8, :] = jnp.maximum(limit_ref[0:8, :], square)

    def mix(u):
        s_ref, w_ref = s_refs[u % 2], w_refs[u % 2]
        for at in range(0, rows, BLK):
            end = at + BLK
            tail = causal(s_ref[at:end, at:end])
            peak = jnp.max(tail, axis=0, keepdims=True)
            if at:
                peak = jnp.maximum(peak, jnp.max(s_ref[:at, at:end], axis=0, keepdims=True))
            e = jnp.exp2((tail - peak) * EXP_SCALE)
            total = jnp.sum(e, axis=0, keepdims=True)
            w_ref[at:end, at:end] = e.astype(BF16)
            if at:
                e = jnp.exp2((s_ref[:at, at:end] - peak) * EXP_SCALE)
                total += jnp.sum(e, axis=0, keepdims=True)
                w_ref[:at, at:end] = e.astype(BF16)
            mixed_ref[u, :, at:end] = dot_nn(vt_ref[:, :end], w_ref[:end, at:end])
            stats_ref[u, 0:1, at:end] = peak
            stats_ref[u, 1:2, at:end] = total
            limit_ref[8:9, at:end] = jnp.maximum(limit_ref[8:9, at:end], -peak)

    for step in range(heads + 1):
        if step < heads:
            scores(step)
        if step:
            mix(step - 1)


def shared_pass(
    lengths_ref, q_ref, g_ref, near_ref, mixed_ref, stats_ref, limit_ref,
    att_ref, qg_ref, back_ref, terms_ref,
    near_wide, k_ref, v_ref, kt_ref, vt_ref, kg_ref, vg_ref, s_refs, dp_refs, w_refs, ds_refs,
    peak_ref, close_ref,
    *, per_group
):
    length = lengths_ref[lax.axis_index("resp")]
    heads = mixed_ref.shape[0]
    rows = q_ref.shape[0]
    groups, near = k_ref.shape[:2]
    senders, chunk = near_ref.shape[:2]
    tokens = near // senders
    steps = per_group // heads
    step_id = pl.program_id(0)
    group = step_id // steps

    @pl.when(step_id == 0)
    def _():
        near_wide[...] = near_ref[...].astype(F32).reshape(senders * chunk, HD)
        for which, (ref, t_ref) in enumerate(((k_ref, kt_ref), (v_ref, vt_ref))):
            for one in range(groups):
                for token in range(tokens):
                    row = (which * groups + one) * tokens + token
                    piece = near_wide[pl.ds(row, senders, stride=chunk), :].astype(BF16)
                    ref[one, token * senders : (token + 1) * senders, :] = piece
                t_ref[one] = ref[one].T
        wide = kt_ref[...].astype(F32)
        longest = jnp.sqrt(jnp.max(jnp.sum(wide * wide, axis=1)) * jnp.max(limit_ref[0:8, :]))
        close_ref[0] = (longest * SLACK + jnp.max(limit_ref[8:9, :]) < REACH).astype(jnp.int32)

    @pl.when(step_id % steps == 0)
    def _():
        kg_ref[...] = jnp.zeros_like(kg_ref)
        vg_ref[...] = jnp.zeros_like(vg_ref)

    @pl.when(close_ref[0] != 0)
    def _():
        for u in range(heads):
            peak_ref[u, 0:1, :] = stats_ref[u, 0:1, :]

    @pl.when(close_ref[0] == 0)
    def _():
        for u in range(heads):
            s = dot_nt(k_ref[group], stacked(q_ref, u))
            peak = jnp.max(s, axis=0, keepdims=True)
            peak_ref[u, 0:1, :] = jnp.maximum(peak, stats_ref[u, 0:1, :])

    inverses, drifts = {}, {}

    def grads(u):
        return live_rows(stacked(g_ref, u), 0, length)

    def scores(u):
        s_refs[u % 3][...] = dot_nt(k_ref[group], stacked(q_ref, u))
        dp_refs[u % 3][...] = dot_nt(v_ref[group], grads(u))

    def mix(u):
        s_ref, w_ref = s_refs[u % 3], w_refs[u % 3]
        peak = peak_ref[u, 0:1, :]
        e = jnp.exp2((s_ref[...] - peak) * EXP_SCALE)
        s_ref[...] = e
        decay = jnp.exp2((stats_ref[u, 0:1, :] - peak) * EXP_SCALE)
        total = jnp.sum(e, axis=0, keepdims=True) + stats_ref[u, 1:2, :] * decay
        inverses[u] = 1.0 / total
        w_ref[...] = (s_ref[...] * inverses[u]).astype(BF16)
        mixed = dot_nn(vt_ref[group], w_ref[...]) + mixed_ref[u] * (decay * inverses[u])
        live = lax.broadcasted_iota(jnp.int32, (1, rows), 1) < length
        att_ref[:, u * HD : (u + 1) * HD] = jnp.where(live, mixed, 0.0).T.astype(BF16)
        drifts[u] = jnp.sum(grads(u).T.astype(F32) * mixed, axis=0, keepdims=True)
        back_ref[u, 0:1, :] = peak
        back_ref[u, 1:2, :] = inverses[u]
        back_ref[u, 2:3, :] = drifts[u]

    def spread(u):
        s_ref, dp_ref, w_ref, ds_ref = s_refs[u % 3], dp_refs[u % 3], w_refs[u % 3], ds_refs[u % 2]
        ds = s_ref[...] * (dp_ref[...] - drifts[u]) * (inverses[u] * SCALE)
        ds_ref[...] = ds.astype(BF16)
        qg_ref[u] = dot_nn(kt_ref[group], ds_ref[...])
        kg_ref[...] += dot_nn(ds_ref[...], stacked(q_ref, u))
        vg_ref[...] += dot_nn(w_ref[...], grads(u))

    for step in range(heads + 2):
        if step < heads:
            scores(step)
        if 0 <= step - 1 < heads:
            mix(step - 1)
        if step >= 2:
            spread(step - 2)

    for one in range(groups):
        @pl.when(step_id == (one + 1) * steps - 1)
        def _():
            for which, ref in enumerate((kg_ref, vg_ref)):
                for token in range(tokens):
                    row = (which * groups + one) * tokens + token
                    near_wide[pl.ds(row, senders, stride=chunk), :] = ref[
                        token * senders : (token + 1) * senders, :
                    ]

    @pl.when(step_id == groups * steps - 1)
    def _():
        terms_ref[...] = near_wide[...].reshape(senders, chunk, HD).astype(BF16)


def own_backward(
    lengths_ref, q_ref, g_ref, k_ref, v_ref, part_ref, back_ref,
    qg_ref, kg_ref, vg_ref, kt_ref, kacc_ref, vacc_ref, s_refs, dp_refs, w_refs, ds_refs,
    *, per_group
):
    length = lengths_ref[lax.axis_index("resp")]
    heads = part_ref.shape[0]
    rows = q_ref.shape[0]
    steps = per_group // heads
    turn = pl.program_id(0) % steps

    @pl.when(turn == 0)
    def _():
        kt_ref[...] = k_ref[...].T
        kacc_ref[...] = jnp.zeros_like(kacc_ref)
        vacc_ref[...] = jnp.zeros_like(vacc_ref)

    def scores(u):
        q = stacked(q_ref, u)
        g = live_rows(stacked(g_ref, u), 0, length)
        for at in range(0, rows, BLK):
            end = at + BLK
            s_refs[u % 2][:end, at:end] = dot_nt(k_ref[:end, :], q[at:end])
            dp_refs[u % 2][:end, at:end] = dot_nt(v_ref[:end, :], g[at:end])

    def spread(u):
        s_ref, dp_ref, w_ref, ds_ref = (refs[u % 2] for refs in (s_refs, dp_refs, w_refs, ds_refs))
        q = stacked(q_ref, u)
        g = live_rows(stacked(g_ref, u), 0, length)
        for at in range(0, rows, BLK):
            end = at + BLK
            peak = back_ref[u, 0:1, at:end]
            inverse = back_ref[u, 1:2, at:end]
            drift = back_ref[u, 2:3, at:end]
            for low in range(0, end, BLK):
                keys = slice(low, low + BLK)
                s = s_ref[keys, at:end]
                if low == at:
                    s = causal(s)
                p = jnp.exp2((s - peak) * EXP_SCALE) * inverse
                w_ref[keys, at:end] = p.astype(BF16)
                ds_ref[keys, at:end] = (p * (dp_ref[keys, at:end] - drift) * SCALE).astype(BF16)
            qg = dot_nn(kt_ref[:, :end], ds_ref[:end, at:end]) + part_ref[u, :, at:end]
            qg_ref[at:end, u * HD : (u + 1) * HD] = qg.T.astype(BF16)
        for low in range(0, rows, BLK):
            keys = slice(low, low + BLK)
            kacc_ref[keys, :] += dot_nn(ds_ref[keys, low:], q[low:])
            vacc_ref[keys, :] += dot_nn(w_ref[keys, low:], g[low:])

    for step in range(heads + 1):
        if step < heads:
            scores(step)
        if step:
            spread(step - 1)

    @pl.when(turn == steps - 1)
    def _():
        kg_ref[...] = kacc_ref[...].astype(BF16)
        vg_ref[...] = vacc_ref[...].astype(BF16)


def copy_pieces(k_ref, v_ref, out_ref):
    tokens, width = k_ref.shape
    shares, copies = out_ref.shape[:2]
    groups = width // shares // HD
    for share in range(shares):
        parts = []
        for ref in (k_ref, v_ref):
            for one in range(groups):
                at = (share * groups + one) * HD
                parts.append(ref[:, at : at + HD].astype(F32))
        piece = jnp.concatenate(parts, axis=0).astype(BF16)
        out_ref[shares - 1 - share] = jnp.broadcast_to(piece[None], (copies,) + piece.shape)


def add_terms(terms_ref, k_ref, v_ref):
    tokens, width = k_ref.shape
    shares = terms_ref.shape[0]
    groups = width // shares // HD
    for share in range(shares):
        total = jnp.sum(terms_ref[shares - 1 - share].astype(F32), axis=0)
        for which, ref in enumerate((k_ref, v_ref)):
            for one in range(groups):
                row = (which * groups + one) * tokens
                at = (share * groups + one) * HD
                ref[:, at : at + HD] = total[row : row + tokens].astype(BF16)


VMEM_LIMIT = 40 * 2**20
TURN = 4


def params():
    return pltpu.CompilerParams(
        dimension_semantics=("arbitrary",), vmem_limit_bytes=VMEM_LIMIT
    )


def shape(dims, dtype=F32):
    return jax.ShapeDtypeStruct(dims, dtype)


def hbm_shape(dims, dtype=F32):
    return pltpu.HBM(dims, dtype)


def in_hbm(*arrays):
    return tuple(pltpu.with_memory_space_constraint(a, pltpu.HBM) for a in arrays)


def specs(rows, per_group):
    steps = per_group // TURN
    return (
        pl.BlockSpec((rows, TURN * HD), lambda h: (0, h)),
        pl.BlockSpec((rows, HD), lambda h: (0, h // steps)),
        pl.BlockSpec((TURN, HD, rows), lambda h: (h, 0, 0)),
        pl.BlockSpec((TURN, 8, rows), lambda h: (h, 0, 0)),
    )


def cost(heads, rows, keys, matmuls, mib):
    return pl.CostEstimate(
        flops=2 * matmuls * heads * rows * keys * HD,
        bytes_accessed=mib * 2**20,
        transcendentals=heads * rows * keys,
    )


def run_own_forward(q, k, v):
    rows, width = q.shape
    heads, groups = width // HD, k.shape[1] // HD
    head, group, wide, stat = specs(rows, heads // groups)
    return pl.pallas_call(
        functools.partial(own_forward, per_group=heads // groups),
        grid=(heads // TURN,),
        in_specs=[head, group, group],
        out_specs=[wide, stat, pl.BlockSpec((16, rows), lambda h: (0, 0))],
        out_shape=[
            hbm_shape((heads, HD, rows)), hbm_shape((heads, 8, rows)), hbm_shape((16, rows)),
        ],
        scratch_shapes=[
            pltpu.VMEM((HD, rows), BF16),
            [pltpu.VMEM((rows, rows), F32)] * 2,
            [pltpu.VMEM((rows, rows), BF16)] * 2,
        ],
        compiler_params=params(),
        cost_estimate=cost(heads, rows, rows, 2, 8),
        name="own_forward",
    )(q, k, v)


def run_shared(lengths, q, g, arrived, mixed, stats, limit):
    rows, width = q.shape
    heads = width // HD
    senders, chunk = arrived.shape[:2]
    groups = 2
    near = senders * chunk // (2 * groups)
    head, _, wide, stat = specs(rows, heads // groups)
    whole = pl.BlockSpec(arrived.shape, lambda h: (0, 0, 0))
    return pl.pallas_call(
        functools.partial(shared_pass, per_group=heads // groups),
        grid=(heads // TURN,),
        in_specs=[
            pl.BlockSpec(memory_space=pltpu.SMEM), head, head, whole, wide, stat,
            pl.BlockSpec((16, rows), lambda h: (0, 0)),
        ],
        out_specs=[head, wide, stat, whole],
        out_shape=[
            hbm_shape((rows, width), BF16), hbm_shape((heads, HD, rows)),
            hbm_shape((heads, 8, rows)), hbm_shape(arrived.shape, BF16),
        ],
        scratch_shapes=[
            pltpu.VMEM((senders * chunk, HD), F32),
            pltpu.VMEM((groups, near, HD), BF16),
            pltpu.VMEM((groups, near, HD), BF16),
            pltpu.VMEM((groups, HD, near), BF16),
            pltpu.VMEM((groups, HD, near), BF16),
            pltpu.VMEM((near, HD), F32),
            pltpu.VMEM((near, HD), F32),
            [pltpu.VMEM((near, rows), F32)] * 3,
            [pltpu.VMEM((near, rows), F32)] * 3,
            [pltpu.VMEM((near, rows), BF16)] * 3,
            [pltpu.VMEM((near, rows), BF16)] * 2,
            pltpu.VMEM((TURN, 8, rows), F32),
            pltpu.SMEM((1,), jnp.int32),
        ],
        compiler_params=params(),
        cost_estimate=cost(heads, rows, near, 6, 16),
        name="shared_pass",
    )(lengths, q, g, arrived, mixed, stats, limit)


def run_own_backward(lengths, q, g, k, v, part, back):
    rows, width = q.shape
    heads, groups = width // HD, k.shape[1] // HD
    head, group, wide, stat = specs(rows, heads // groups)
    return pl.pallas_call(
        functools.partial(own_backward, per_group=heads // groups),
        grid=(heads // TURN,),
        in_specs=[
            pl.BlockSpec(memory_space=pltpu.SMEM), head, head, group, group, wide, stat
        ],
        out_specs=[head, group, group],
        out_shape=[shape((rows, width), BF16), shape(k.shape, BF16), shape(v.shape, BF16)],
        scratch_shapes=[
            pltpu.VMEM((HD, rows), BF16),
            pltpu.VMEM((rows, HD), F32),
            pltpu.VMEM((rows, HD), F32),
            [pltpu.VMEM((rows, rows), F32)] * 2,
            [pltpu.VMEM((rows, rows), F32)] * 2,
            [pltpu.VMEM((rows, rows), BF16)] * 2,
            [pltpu.VMEM((rows, rows), BF16)] * 2,
        ],
        compiler_params=params(),
        cost_estimate=cost(heads, rows, rows, 5, 12),
        name="own_backward",
    )(lengths, q, g, k, v, part, back)


def on_device(prompt_keys, prompt_values, q, resp_k, resp_v, grad_out, lengths):
    axes = ("prompt", "resp")
    shares = lax.axis_size("prompt")
    copies = lax.axis_size("resp")
    tokens, width = prompt_keys.shape
    chunk = 2 * tokens * width // shares // HD

    prompt_keys, prompt_values = in_hbm(prompt_keys, prompt_values)
    pieces = pl.pallas_call(
        copy_pieces,
        out_shape=shape((shares, copies, chunk, HD), BF16),
        compiler_params=pltpu.CompilerParams(vmem_limit_bytes=VMEM_LIMIT),
        name="copy_pieces",
    )(prompt_keys, prompt_values)
    pieces = pieces.reshape(shares * copies, chunk, HD)
    backward = [list(reversed(range(shares * copies)))]
    arrived = lax.all_to_all(pieces, axes, split_axis=0, concat_axis=0, tiled=True,
        axis_index_groups=backward,
    )

    q, resp_k, resp_v, grad_out = in_hbm(q, resp_k, resp_v, grad_out)
    mixed, stats, limit = in_hbm(*run_own_forward(q, resp_k, resp_v))
    attended, part, back, terms = run_shared(
        lengths, q, grad_out, arrived, mixed, stats, limit
    )
    part, back = in_hbm(part, back)
    terms = lax.all_to_all(terms, axes, split_axis=0, concat_axis=0, tiled=True,
        axis_index_groups=backward,
    )
    query_grads, key_grads, value_grads = run_own_backward(
        lengths, q, grad_out, resp_k, resp_v, part, back
    )
    prompt_kg, prompt_vg = pl.pallas_call(
        add_terms,
        out_shape=[shape((tokens, width), BF16)] * 2,
        compiler_params=pltpu.CompilerParams(vmem_limit_bytes=VMEM_LIMIT),
        name="add_terms",
    )(terms.reshape(shares, copies, chunk, HD))
    return attended, query_grads, key_grads, value_grads, prompt_kg, prompt_vg


def solution(mesh):
    return jax.shard_map(
        on_device,
        mesh=mesh,
        in_specs=(
            P(("prompt", "resp"), None),
            P(("prompt", "resp"), None),
            P("resp", "prompt"),
            P("resp", "prompt"),
            P("resp", "prompt"),
            P("resp", "prompt"),
            P(),
        ),
        out_specs=(
            P("resp", "prompt"),
            P("resp", "prompt"),
            P("resp", "prompt"),
            P("resp", "prompt"),
            P(("prompt", "resp"), None),
            P(("prompt", "resp"), None),
        ),
        check_vma=False,
    )
```

```python
import functools
import math

import jax
import jax.numpy as jnp
from jax import lax
from jax.experimental import pallas as pl
from jax.experimental.pallas import tpu as pltpu
from jax.sharding import PartitionSpec as P

HD = 128
BLK = 256
SCALE = 1.0 / math.sqrt(HD)
EXP_SCALE = SCALE * math.log2(math.e)
NEG = -1e30
REACH = 100 / EXP_SCALE
SLACK = 1.02
F32 = jnp.float32
BF16 = jnp.bfloat16


def dot_nt(a, b):
    return lax.dot_general(a, b, (((1,), (1,)), ((), ())), preferred_element_type=F32)


def dot_nn(a, b):
    return lax.dot_general(a, b, (((1,), (0,)), ((), ())), preferred_element_type=F32)


def live_rows(block, start, length):
    parts = []
    for at in range(0, block.shape[0], HD):
        factor = (start + at < length).astype(F32).astype(BF16)
        parts.append(block[at : at + HD] * factor)
    return jnp.concatenate(parts, axis=0)


def causal(s):
    key = lax.broadcasted_iota(jnp.int32, s.shape, 0)
    query = lax.broadcasted_iota(jnp.int32, s.shape, 1)
    return jnp.where(key <= query, s, NEG)


def stacked(ref, head):
    return ref[:, head * HD : (head + 1) * HD]


def own_forward(
    q_ref, k_ref, v_ref, mixed_ref, stats_ref, limit_ref, vt_ref, s_refs, w_refs, *, per_group
):
    heads = mixed_ref.shape[0]
    rows = q_ref.shape[0]

    @pl.when(pl.program_id(0) % (per_group // heads) == 0)
    def _():
        vt_ref[...] = v_ref[...].T

    @pl.when(pl.program_id(0) == 0)
    def _():
        limit_ref[...] = jnp.full(limit_ref.shape, NEG, F32)

    def scores(u):
        q = stacked(q_ref, u)
        for at in range(0, rows, BLK):
            end = at + BLK
            s_refs[u % 2][:end, at:end] = dot_nt(k_ref[:end, :], q[at:end])
        square = dot_nt(jnp.ones((8, HD), BF16), q * q)
        limit_ref[0:8, :] = jnp.maximum(limit_ref[0:8, :], square)

    def mix(u):
        s_ref, w_ref = s_refs[u % 2], w_refs[u % 2]
        for at in range(0, rows, BLK):
            end = at + BLK
            tail = causal(s_ref[at:end, at:end])
            peak = jnp.max(tail, axis=0, keepdims=True)
            if at:
                peak = jnp.maximum(peak, jnp.max(s_ref[:at, at:end], axis=0, keepdims=True))
            e = jnp.exp2((tail - peak) * EXP_SCALE)
            total = jnp.sum(e, axis=0, keepdims=True)
            w_ref[at:end, at:end] = e.astype(BF16)
            if at:
                e = jnp.exp2((s_ref[:at, at:end] - peak) * EXP_SCALE)
                total += jnp.sum(e, axis=0, keepdims=True)
                w_ref[:at, at:end] = e.astype(BF16)
            mixed_ref[u, :, at:end] = dot_nn(vt_ref[:, :end], w_ref[:end, at:end])
            stats_ref[u, 0:1, at:end] = peak
            stats_ref[u, 1:2, at:end] = total
            limit_ref[8:9, at:end] = jnp.maximum(limit_ref[8:9, at:end], -peak)

    for step in range(heads + 1):
        if step < heads:
            scores(step)
        if step:
            mix(step - 1)


def shared_pass(
    lengths_ref, q_ref, g_ref, near_ref, mixed_ref, stats_ref, limit_ref,
    att_ref, qg_ref, back_ref, terms_ref,
    near_wide, k_ref, v_ref, kt_ref, vt_ref, kg_ref, vg_ref, s_refs, dp_refs, w_refs, ds_refs,
    peak_ref, close_ref,
    *, per_group
):
    length = lengths_ref[lax.axis_index("resp")]
    heads = mixed_ref.shape[0]
    rows = q_ref.shape[0]
    groups, near = k_ref.shape[:2]
    senders, chunk = near_ref.shape[:2]
    tokens = near // senders
    steps = per_group // heads
    step_id = pl.program_id(0)
    group = step_id // steps

    @pl.when(step_id == 0)
    def _():
        near_wide[...] = near_ref[...].astype(F32).reshape(senders * chunk, HD)
        for which, (ref, t_ref) in enumerate(((k_ref, kt_ref), (v_ref, vt_ref))):
            for one in range(groups):
                for token in range(tokens):
                    row = (which * groups + one) * tokens + token
                    piece = near_wide[pl.ds(row, senders, stride=chunk), :].astype(BF16)
                    ref[one, token * senders : (token + 1) * senders, :] = piece
                t_ref[one] = ref[one].T
        wide = kt_ref[...].astype(F32)
        longest = jnp.sqrt(jnp.max(jnp.sum(wide * wide, axis=1)) * jnp.max(limit_ref[0:8, :]))
        close_ref[0] = (longest * SLACK + jnp.max(limit_ref[8:9, :]) < REACH).astype(jnp.int32)

    @pl.when(step_id % steps == 0)
    def _():
        kg_ref[...] = jnp.zeros_like(kg_ref)
        vg_ref[...] = jnp.zeros_like(vg_ref)

    @pl.when(close_ref[0] != 0)
    def _():
        for u in range(heads):
            peak_ref[u, 0:1, :] = stats_ref[u, 0:1, :]

    @pl.when(close_ref[0] == 0)
    def _():
        for u in range(heads):
            s = dot_nt(k_ref[group], stacked(q_ref, u))
            peak = jnp.max(s, axis=0, keepdims=True)
            peak_ref[u, 0:1, :] = jnp.maximum(peak, stats_ref[u, 0:1, :])

    inverses, drifts = {}, {}

    def grads(u):
        return live_rows(stacked(g_ref, u), 0, length)

    def scores(u):
        s_refs[u % 3][...] = dot_nt(k_ref[group], stacked(q_ref, u))
        dp_refs[u % 3][...] = dot_nt(v_ref[group], grads(u))

    def mix(u):
        s_ref, w_ref = s_refs[u % 3], w_refs[u % 3]
        peak = peak_ref[u, 0:1, :]
        e = jnp.exp2((s_ref[...] - peak) * EXP_SCALE)
        s_ref[...] = e
        decay = jnp.exp2((stats_ref[u, 0:1, :] - peak) * EXP_SCALE)
        total = jnp.sum(e, axis=0, keepdims=True) + stats_ref[u, 1:2, :] * decay
        inverses[u] = 1.0 / total
        w_ref[...] = (s_ref[...] * inverses[u]).astype(BF16)
        mixed = dot_nn(vt_ref[group], w_ref[...]) + mixed_ref[u] * (decay * inverses[u])
        live = lax.broadcasted_iota(jnp.int32, (1, rows), 1) < length
        att_ref[:, u * HD : (u + 1) * HD] = jnp.where(live, mixed, 0.0).T.astype(BF16)
        drifts[u] = jnp.sum(grads(u).T.astype(F32) * mixed, axis=0, keepdims=True)
        back_ref[u, 0:1, :] = peak
        back_ref[u, 1:2, :] = inverses[u]
        back_ref[u, 2:3, :] = drifts[u]

    def spread(u):
        s_ref, dp_ref, w_ref, ds_ref = s_refs[u % 3], dp_refs[u % 3], w_refs[u % 3], ds_refs[u % 2]
        ds = s_ref[...] * (dp_ref[...] - drifts[u]) * (inverses[u] * SCALE)
        ds_ref[...] = ds.astype(BF16)
        qg_ref[u] = dot_nn(kt_ref[group], ds_ref[...])
        kg_ref[...] += dot_nn(ds_ref[...], stacked(q_ref, u))
        vg_ref[...] += dot_nn(w_ref[...], grads(u))

    for step in range(heads + 2):
        if step < heads:
            scores(step)
        if 0 <= step - 1 < heads:
            mix(step - 1)
        if step >= 2:
            spread(step - 2)

    for one in range(groups):
        @pl.when(step_id == (one + 1) * steps - 1)
        def _():
            for which, ref in enumerate((kg_ref, vg_ref)):
                for token in range(tokens):
                    row = (which * groups + one) * tokens + token
                    near_wide[pl.ds(row, senders, stride=chunk), :] = ref[
                        token * senders : (token + 1) * senders, :
                    ]

    @pl.when(step_id == groups * steps - 1)
    def _():
        terms_ref[...] = near_wide[...].reshape(senders, chunk, HD).astype(BF16)


def own_backward(
    lengths_ref, q_ref, g_ref, k_ref, v_ref, part_ref, back_ref,
    qg_ref, kg_ref, vg_ref, kt_ref, kacc_ref, vacc_ref, s_refs, dp_refs, w_refs, ds_refs,
    *, per_group
):
    length = lengths_ref[lax.axis_index("resp")]
    heads = part_ref.shape[0]
    rows = q_ref.shape[0]
    steps = per_group // heads
    turn = pl.program_id(0) % steps

    @pl.when(turn == 0)
    def _():
        kt_ref[...] = k_ref[...].T
        kacc_ref[...] = jnp.zeros_like(kacc_ref)
        vacc_ref[...] = jnp.zeros_like(vacc_ref)

    def scores(u):
        q = stacked(q_ref, u)
        g = live_rows(stacked(g_ref, u), 0, length)
        for at in range(0, rows, BLK):
            end = at + BLK
            s_refs[u % 2][:end, at:end] = dot_nt(k_ref[:end, :], q[at:end])
            dp_refs[u % 2][:end, at:end] = dot_nt(v_ref[:end, :], g[at:end])

    def spread(u):
        s_ref, dp_ref, w_ref, ds_ref = (refs[u % 2] for refs in (s_refs, dp_refs, w_refs, ds_refs))
        q = stacked(q_ref, u)
        g = live_rows(stacked(g_ref, u), 0, length)
        for at in range(0, rows, BLK):
            end = at + BLK
            peak = back_ref[u, 0:1, at:end]
            inverse = back_ref[u, 1:2, at:end]
            drift = back_ref[u, 2:3, at:end]
            for low in range(0, end, BLK):
                keys = slice(low, low + BLK)
                s = s_ref[keys, at:end]
                if low == at:
                    s = causal(s)
                p = jnp.exp2((s - peak) * EXP_SCALE) * inverse
                w_ref[keys, at:end] = p.astype(BF16)
                ds_ref[keys, at:end] = (p * (dp_ref[keys, at:end] - drift) * SCALE).astype(BF16)
            qg = dot_nn(kt_ref[:, :end], ds_ref[:end, at:end]) + part_ref[u, :, at:end]
            qg_ref[at:end, u * HD : (u + 1) * HD] = qg.T.astype(BF16)
        for low in range(0, rows, BLK):
            keys = slice(low, low + BLK)
            kacc_ref[keys, :] += dot_nn(ds_ref[keys, low:], q[low:])
            vacc_ref[keys, :] += dot_nn(w_ref[keys, low:], g[low:])

    for step in range(heads + 1):
        if step < heads:
            scores(step)
        if step:
            spread(step - 1)

    @pl.when(turn == steps - 1)
    def _():
        kg_ref[...] = kacc_ref[...].astype(BF16)
        vg_ref[...] = vacc_ref[...].astype(BF16)


def copy_pieces(k_ref, v_ref, out_ref):
    tokens, width = k_ref.shape
    copies, shares = out_ref.shape[:2]
    groups = width // shares // HD
    for share in range(shares):
        parts = []
        for ref in (k_ref, v_ref):
            for one in range(groups):
                at = (share * groups + one) * HD
                parts.append(ref[:, at : at + HD].astype(F32))
        piece = jnp.concatenate(parts, axis=0).astype(BF16)
        out_ref[:, shares - 1 - share] = jnp.broadcast_to(piece[None], (copies,) + piece.shape)


def add_terms(terms_ref, k_ref, v_ref):
    tokens, width = k_ref.shape
    shares = terms_ref.shape[1]
    groups = width // shares // HD
    for share in range(shares):
        total = jnp.sum(terms_ref[:, shares - 1 - share].astype(F32), axis=0)
        for which, ref in enumerate((k_ref, v_ref)):
            for one in range(groups):
                row = (which * groups + one) * tokens
                at = (share * groups + one) * HD
                ref[:, at : at + HD] = total[row : row + tokens].astype(BF16)


VMEM_LIMIT = 40 * 2**20
TURN = 4


def params():
    return pltpu.CompilerParams(
        dimension_semantics=("arbitrary",), vmem_limit_bytes=VMEM_LIMIT
    )


def shape(dims, dtype=F32):
    return jax.ShapeDtypeStruct(dims, dtype)


def hbm_shape(dims, dtype=F32):
    return pltpu.HBM(dims, dtype)


def in_hbm(*arrays):
    return tuple(pltpu.with_memory_space_constraint(a, pltpu.HBM) for a in arrays)


def specs(rows, per_group):
    steps = per_group // TURN
    return (
        pl.BlockSpec((rows, TURN * HD), lambda h: (0, h)),
        pl.BlockSpec((rows, HD), lambda h: (0, h // steps)),
        pl.BlockSpec((TURN, HD, rows), lambda h: (h, 0, 0)),
        pl.BlockSpec((TURN, 8, rows), lambda h: (h, 0, 0)),
    )


def cost(heads, rows, keys, matmuls, mib):
    return pl.CostEstimate(
        flops=2 * matmuls * heads * rows * keys * HD,
        bytes_accessed=mib * 2**20,
        transcendentals=heads * rows * keys,
    )


def run_own_forward(q, k, v):
    rows, width = q.shape
    heads, groups = width // HD, k.shape[1] // HD
    head, group, wide, stat = specs(rows, heads // groups)
    return pl.pallas_call(
        functools.partial(own_forward, per_group=heads // groups),
        grid=(heads // TURN,),
        in_specs=[head, group, group],
        out_specs=[wide, stat, pl.BlockSpec((16, rows), lambda h: (0, 0))],
        out_shape=[
            hbm_shape((heads, HD, rows)), hbm_shape((heads, 8, rows)), hbm_shape((16, rows)),
        ],
        scratch_shapes=[
            pltpu.VMEM((HD, rows), BF16),
            [pltpu.VMEM((rows, rows), F32)] * 2,
            [pltpu.VMEM((rows, rows), BF16)] * 2,
        ],
        compiler_params=params(),
        cost_estimate=cost(heads, rows, rows, 2, 8),
        name="own_forward",
    )(q, k, v)


def run_shared(lengths, q, g, arrived, mixed, stats, limit):
    rows, width = q.shape
    heads = width // HD
    senders, chunk = arrived.shape[:2]
    groups = 2
    near = senders * chunk // (2 * groups)
    head, _, wide, stat = specs(rows, heads // groups)
    whole = pl.BlockSpec(arrived.shape, lambda h: (0, 0, 0))
    return pl.pallas_call(
        functools.partial(shared_pass, per_group=heads // groups),
        grid=(heads // TURN,),
        in_specs=[
            pl.BlockSpec(memory_space=pltpu.SMEM), head, head, whole, wide, stat,
            pl.BlockSpec((16, rows), lambda h: (0, 0)),
        ],
        out_specs=[head, wide, stat, whole],
        out_shape=[
            hbm_shape((rows, width), BF16), hbm_shape((heads, HD, rows)),
            hbm_shape((heads, 8, rows)), hbm_shape(arrived.shape, BF16),
        ],
        scratch_shapes=[
            pltpu.VMEM((senders * chunk, HD), F32),
            pltpu.VMEM((groups, near, HD), BF16),
            pltpu.VMEM((groups, near, HD), BF16),
            pltpu.VMEM((groups, HD, near), BF16),
            pltpu.VMEM((groups, HD, near), BF16),
            pltpu.VMEM((near, HD), F32),
            pltpu.VMEM((near, HD), F32),
            [pltpu.VMEM((near, rows), F32)] * 3,
            [pltpu.VMEM((near, rows), F32)] * 3,
            [pltpu.VMEM((near, rows), BF16)] * 3,
            [pltpu.VMEM((near, rows), BF16)] * 2,
            pltpu.VMEM((TURN, 8, rows), F32),
            pltpu.SMEM((1,), jnp.int32),
        ],
        compiler_params=params(),
        cost_estimate=cost(heads, rows, near, 6, 16),
        name="shared_pass",
    )(lengths, q, g, arrived, mixed, stats, limit)


def run_own_backward(lengths, q, g, k, v, part, back):
    rows, width = q.shape
    heads, groups = width // HD, k.shape[1] // HD
    head, group, wide, stat = specs(rows, heads // groups)
    return pl.pallas_call(
        functools.partial(own_backward, per_group=heads // groups),
        grid=(heads // TURN,),
        in_specs=[
            pl.BlockSpec(memory_space=pltpu.SMEM), head, head, group, group, wide, stat
        ],
        out_specs=[head, group, group],
        out_shape=[shape((rows, width), BF16), shape(k.shape, BF16), shape(v.shape, BF16)],
        scratch_shapes=[
            pltpu.VMEM((HD, rows), BF16),
            pltpu.VMEM((rows, HD), F32),
            pltpu.VMEM((rows, HD), F32),
            [pltpu.VMEM((rows, rows), F32)] * 2,
            [pltpu.VMEM((rows, rows), F32)] * 2,
            [pltpu.VMEM((rows, rows), BF16)] * 2,
            [pltpu.VMEM((rows, rows), BF16)] * 2,
        ],
        compiler_params=params(),
        cost_estimate=cost(heads, rows, rows, 5, 12),
        name="own_backward",
    )(lengths, q, g, k, v, part, back)


def on_device(prompt_keys, prompt_values, q, resp_k, resp_v, grad_out, lengths):
    axes = ("prompt", "resp")
    shares = lax.axis_size("prompt")
    copies = lax.axis_size("resp")
    tokens, width = prompt_keys.shape
    chunk = 2 * tokens * width // shares // HD

    prompt_keys, prompt_values = in_hbm(prompt_keys, prompt_values)
    pieces = pl.pallas_call(
        copy_pieces,
        out_shape=shape((copies, shares, chunk, HD), BF16),
        compiler_params=pltpu.CompilerParams(vmem_limit_bytes=VMEM_LIMIT),
        name="copy_pieces",
    )(prompt_keys, prompt_values)
    pieces = pieces.reshape(shares * copies, chunk, HD)
    backward = [
        [p * copies + r for r in reversed(range(copies)) for p in reversed(range(shares))]
    ]
    arrived = lax.all_to_all(pieces, axes, split_axis=0, concat_axis=0, tiled=True,
        axis_index_groups=backward,
    )

    q, resp_k, resp_v, grad_out = in_hbm(q, resp_k, resp_v, grad_out)
    mixed, stats, limit = in_hbm(*run_own_forward(q, resp_k, resp_v))
    attended, part, back, terms = run_shared(
        lengths, q, grad_out, arrived, mixed, stats, limit
    )
    part, back = in_hbm(part, back)
    terms = lax.all_to_all(terms, axes, split_axis=0, concat_axis=0, tiled=True,
        axis_index_groups=backward,
    )
    query_grads, key_grads, value_grads = run_own_backward(
        lengths, q, grad_out, resp_k, resp_v, part, back
    )
    prompt_kg, prompt_vg = pl.pallas_call(
        add_terms,
        out_shape=[shape((tokens, width), BF16)] * 2,
        compiler_params=pltpu.CompilerParams(vmem_limit_bytes=VMEM_LIMIT),
        name="add_terms",
    )(terms.reshape(copies, shares, chunk, HD))
    return attended, query_grads, key_grads, value_grads, prompt_kg, prompt_vg


def solution(mesh):
    return jax.shard_map(
        on_device,
        mesh=mesh,
        in_specs=(
            P(("prompt", "resp"), None),
            P(("prompt", "resp"), None),
            P("resp", "prompt"),
            P("resp", "prompt"),
            P("resp", "prompt"),
            P("resp", "prompt"),
            P(),
        ),
        out_specs=(
            P("resp", "prompt"),
            P("resp", "prompt"),
            P("resp", "prompt"),
            P("resp", "prompt"),
            P(("prompt", "resp"), None),
            P(("prompt", "resp"), None),
        ),
        check_vma=False,
    )
```
